128 devices in a mesh: seq: 8 (over z, core), head: 16 (over y, x).
Axes of the slice: x: 4, y: 4, z: 4, core: 2. Of those that a mesh axis runs over, the one named last changes fastest.
Arguments:
- tokens: bfloat16 [2, 2048, 2048], P(None, 'seq', 'head'), may hold values from -6 to 6
- attn_gain: float32 [2048], replicated, may hold values from 0.1 to 1.9
- w_query: bfloat16 [2048, 4096], P(None, 'head'), may hold values from -0.125 to 0.125
- w_key: bfloat16 [2048, 4096], P(None, 'head'), may hold values from -0.125 to 0.125
- w_value: bfloat16 [2048, 4096], P(None, 'head'), may hold values from -0.125 to 0.125
- w_gate: bfloat16 [2048, 4096], P(None, 'head'), may hold values from -0.125 to 0.125
- head_gain: float32 [4096], P('head'), may hold values from 0.1 to 1.9
- w_out: bfloat16 [4096, 2048], P('head'), may hold values from -0.09375 to 0.09375
- moe_gain: float32 [2048], replicated, may hold values from 0.1 to 1.9
- w_router: bfloat16 [2048, 128], replicated, may hold values from -0.125 to 0.125
- expert_picks: int32 [8, 512, 8], P('seq', 'head'), may hold values from 0 to 127, all different within a row; in each aligned block of 32 rows (0 to 31, 32 to 63, ..., all dimensions but the last counted through in order) at most 3 rows name the same one
- exp_gate: bfloat16 [128, 2048, 768], P(('seq', 'head')), may hold values from -0.125 to 0.125
- exp_up: bfloat16 [128, 2048, 768], P(('seq', 'head')), may hold values from -0.125 to 0.125
- exp_down: bfloat16 [128, 768, 2048], P(('seq', 'head')), may hold values from -0.21875 to 0.21875
Outputs:
- layer_out: float32 [8, 512, 2048], P('seq', 'head')
The draws below stay inside these ranges and needn't reach their ends.
Inputs may be any that keep to these rules, and one draw needn't show every extreme that they name: `expert_picks`: each row names 8 different experts. In each aligned block of 32 rows no expert is named by more than 3 rows, a bound that some block reaches.
All inputs are finite; a program needn't handle non-finite values.
Results may differ from the reference program's by a relative error of at most 0.007.
Values may be sent and summed in bfloat16 or wider, within the bound.
A program may use at most 64 MiB of HBM per device.

```python
import math
import jax
import jax.numpy as jnp
import numpy as np
from jax import lax

D = 2048
HEADS = 32
DH = 128
FF = 768
TOP = 8
BLOCK = 256
SEQS = 2
LEN_DEV = 256
LEN = 2048
ROWS = 32
EXPERTS = 128
MOST = 3
N_SEQ = 8


def level_of(own_key, dims, shards, low, high):
    def one(dim, shards_of):
        draws = jax.random.uniform(jax.random.fold_in(jax.random.fold_in(own_key, 6), dim), (shards_of,), jnp.float32, low / len(shards), high / len(shards))
        return jnp.repeat(jnp.exp(draws), dims[dim] // shards_of).reshape((-1,) + (1,) * (len(dims) - dim - 1))

    level = one(*shards[0])
    for cut in shards[1:]:
        level = level * one(*cut)
    return level


def assign_block(key, own, number, rows, count, top, reach, slope):
    order = jax.random.permutation(key, count)
    crowded, usual = portions_of(count, rows * top, reach, slope, True), portions_of(count, rows * top, reach, slope, False)
    places = jnp.arange(count)

    def named(tallies, offset_by):
        used = int((tallies > 0).sum())
        fixed = max(1, used // 4)
        moved = fixed + (places - fixed + offset_by * (used - fixed)) % max(1, count - fixed)
        return jnp.zeros((count,), jnp.int32).at[order[jnp.where(places < fixed, places, moved)]].set(jnp.asarray(tallies, jnp.int32))

    tallies = jnp.where(number % 4 == 0, named(crowded, number // 4), named(usual, number - number // 4 - 1))
    mixed = jax.random.permutation(jax.random.fold_in(own, 3), count)
    giver, sink = mixed[0:count // 2 * 2:2], mixed[1:count // 2 * 2:2]
    room = jnp.minimum(tallies[giver] - 1, reach - tallies[sink]) // 2
    room = jnp.where((giver == order[0]) | (sink == order[0]) | (tallies[sink] == 0), 0, jnp.maximum(room, 0))
    moved = jax.random.randint(jax.random.fold_in(own, 4), (count // 2,), 0, 1 << 20) % (room + 1)
    tallies = tallies.at[giver].add(-moved).at[sink].add(moved)
    labels = jnp.searchsorted(jnp.cumsum(tallies), jnp.arange(rows * top), side="right").astype(jnp.int32)
    listing = labels.reshape(top, rows).T
    listing = listing[jax.random.permutation(jax.random.fold_in(own, 1), rows)]
    offset_by = jax.random.randint(jax.random.fold_in(own, 2), (rows, 1), 0, top)
    return jnp.take_along_axis(listing, (jnp.arange(top)[None, :] + offset_by) % top, axis=1)


def portions_of(number_of, total, reach, slope, full):
    portions = [(1 << 20) // math.isqrt(standing ** slope) + 1 for standing in range(1, number_of + 1)]
    largest = reach if full else min(reach, max(-(-total // number_of), total * portions[0] // sum(portions)))
    least = 1 if total - largest >= number_of - 1 else 0
    holding, spare = [largest] + [least] * (number_of - 1), total - largest - least * (number_of - 1)
    while spare > 0:
        movable = [i for i in range(1, number_of) if holding[i] < largest] or [i for i in range(1, number_of) if holding[i] < reach]
        mass, left = sum([portions[i] for i in movable]), spare
        for i in movable:
            more = min(reach - holding[i], max(1, left * portions[i] // mass), spare)
            holding[i] = holding[i] + more
            spare = spare - more
    return np.array(holding)


def noise(stream_key, shape, scale, most, pieces=(), kind=jnp.bfloat16):
    entries = jax.random.normal(stream_key, shape, jnp.float32) * scale
    if len(pieces) > 0:
        entries = level_of(stream_key, shape, pieces, -0.22, 0.18) * entries
    return jnp.clip(entries, min=-most, max=most).astype(kind)


def setup_inputs(seed: int = 0) -> dict:
    seeds = jax.random.split(jax.random.key(seed), 15)
    tokens = noise(seeds[0], (SEQS, LEN, D), 1.0, 6.0, ((1, 8), (2, 16)))
    attn_gain = jnp.clip(1.0 + 0.18 * jax.random.normal(seeds[1], (D,), jnp.float32), 0.1, 1.9)
    w_query = noise(seeds[2], (D, HEADS * DH), D ** -0.5, 0.125, ((1, 16),))
    w_key = noise(seeds[3], (D, HEADS * DH), D ** -0.5, 0.125, ((1, 16),))
    w_value = noise(seeds[4], (D, HEADS * DH), D ** -0.5, 0.125, ((1, 16),))
    w_gate = noise(seeds[5], (D, HEADS * DH), D ** -0.5, 0.125, ((1, 16),))
    head_gain = jnp.clip(1.0 + 0.18 * jax.random.normal(seeds[6], (HEADS * DH,), jnp.float32), 0.1, 1.9)
    w_out = noise(seeds[7], (HEADS * DH, D), (HEADS * DH) ** -0.5, 0.09375, ((0, 16),))
    moe_gain = jnp.clip(1.0 + 0.18 * jax.random.normal(seeds[8], (D,), jnp.float32), 0.1, 1.9)
    w_router = noise(seeds[9], (D, EXPERTS), D ** -0.5, 0.125)
    expert_picks_keys = jax.random.split(jax.random.fold_in(seeds[10], 1), N_SEQ * (SEQS * LEN_DEV) // ROWS)
    expert_picks_turns = jax.random.permutation(jax.random.fold_in(seeds[10], 3), N_SEQ * (SEQS * LEN_DEV) // ROWS)
    expert_picks = jax.vmap(lambda own, number: assign_block(jax.random.fold_in(seeds[10], 2), own, number, ROWS, EXPERTS, TOP, MOST, 2))(expert_picks_keys, expert_picks_turns).reshape((N_SEQ, SEQS * LEN_DEV, TOP))
    exp_gate = noise(seeds[11], (EXPERTS, D, FF), D ** -0.5, 0.125, ((0, 128),))
    exp_up = noise(seeds[12], (EXPERTS, D, FF), D ** -0.5, 0.125, ((0, 128),))
    exp_down = noise(seeds[13], (EXPERTS, FF, D), FF ** -0.5, 0.21875, ((0, 128),))
    return {"tokens": tokens, "attn_gain": attn_gain, "w_query": w_query, "w_key": w_key, "w_value": w_value, "w_gate": w_gate, "head_gain": head_gain, "w_out": w_out, "moe_gain": moe_gain, "w_router": w_router, "expert_picks": expert_picks, "exp_gate": exp_gate, "exp_up": exp_up, "exp_down": exp_down}


epsilon = 1e-06

def rms_scale(values, gain_vec):
    mean_sq = lax.optimization_barrier(jnp.mean(values * values, axis=-1, keepdims=True))
    return values * lax.rsqrt(mean_sq + epsilon) * gain_vec

def expert_rows(inputs, gate_weight, up_weight, down_weight):
    gate_act = jnp.dot(inputs, gate_weight, preferred_element_type=jnp.float32)
    up_act = jnp.dot(inputs, up_weight, preferred_element_type=jnp.float32)
    hidden = (jax.nn.silu(gate_act) * up_act).astype(jnp.bfloat16)
    return jnp.dot(hidden, down_weight, preferred_element_type=jnp.float32).astype(jnp.bfloat16)

def reference(tokens, attn_gain, w_query, w_key, w_value, w_gate, head_gain, w_out, moe_gain, w_router, expert_picks, exp_gate, exp_up, exp_down):
    seq_count, length, model_width = tokens.shape
    block_count = length // BLOCK
    normed = rms_scale(tokens.astype(jnp.float32), attn_gain).astype(jnp.bfloat16).reshape(seq_count * length, model_width)
    heads_query = w_query.reshape(model_width, HEADS, DH).transpose(1, 0, 2)
    heads_key = w_key.reshape(model_width, HEADS, DH).transpose(1, 0, 2)
    heads_value = w_value.reshape(model_width, HEADS, DH).transpose(1, 0, 2)
    heads_gate = w_gate.reshape(model_width, HEADS, DH).transpose(1, 0, 2)
    heads_gain = head_gain.reshape(HEADS, DH)
    heads_out = w_out.reshape(HEADS, DH, model_width)
    causal = jnp.arange(BLOCK)[:, None] >= jnp.arange(BLOCK)[None, :]

    def head_step(running, stacked):
        query_w, key_w, value_w, gate_weight, gain_vec, out_weight = stacked

        def project(weight):
            return jnp.dot(normed, weight, preferred_element_type=jnp.float32)
        block_shape = (seq_count, block_count, BLOCK, DH)
        query_act = jax.nn.silu(project(query_w)).astype(jnp.bfloat16).reshape(block_shape).astype(jnp.float32)
        key_act = jax.nn.silu(project(key_w)).astype(jnp.bfloat16).reshape(block_shape).astype(jnp.float32)
        value_act = jax.nn.silu(project(value_w)).astype(jnp.bfloat16).reshape(block_shape).astype(jnp.float32)
        gate_out = jax.nn.sigmoid(project(gate_weight))
        scores = jnp.einsum('snid,snjd->snij', query_act, key_act)
        scores = jnp.where(causal, scores, 0.0).astype(jnp.bfloat16).astype(jnp.float32)
        inner_part = jnp.einsum('snij,snjd->snid', scores, value_act)
        block_states = jnp.einsum('snjd,snje->snde', key_act, value_act)
        prefix = (jnp.cumsum(block_states, axis=1) - block_states).astype(jnp.bfloat16).astype(jnp.float32)
        outer_part = jnp.einsum('snid,snde->snie', query_act, prefix)
        mixed = (inner_part + outer_part).reshape(seq_count * length, DH)
        gated_out = (rms_scale(mixed, gain_vec) * gate_out).astype(jnp.bfloat16)
        return (running + jnp.dot(gated_out, out_weight, preferred_element_type=jnp.float32), None)
    attention, ignored = lax.scan(head_step, jnp.zeros((seq_count * length, model_width), jnp.float32), (heads_query, heads_key, heads_value, heads_gate, heads_gain, heads_out))
    residual_full = tokens.astype(jnp.float32) + attention.reshape(seq_count, length, model_width)
    residual = residual_full.reshape(seq_count, N_SEQ, LEN_DEV, model_width).transpose(1, 0, 2, 3).reshape(EXPERTS, ROWS, model_width)
    moe_in = rms_scale(residual, moe_gain).astype(jnp.bfloat16)
    logits = jnp.einsum('nrd,de->nre', moe_in.astype(jnp.float32), w_router.astype(jnp.float32))
    chosen = expert_picks.reshape(EXPERTS, ROWS, TOP).astype(jnp.int32)
    picked = jnp.take_along_axis(logits, chosen, axis=2)
    pick_scores = jax.nn.sigmoid(picked)
    weights = pick_scores / lax.optimization_barrier(jnp.sum(pick_scores, axis=2, keepdims=True))
    expert_of = chosen.reshape(EXPERTS, ROWS * TOP)
    one_hot = (expert_of[:, :, None] == jnp.arange(EXPERTS, dtype=jnp.int32)[None, None, :]).astype(jnp.int32)
    before = (jnp.cumsum(one_hot, axis=1) - one_hot).astype(jnp.int32)
    slot_index = lax.optimization_barrier(jnp.sum(before * one_hot, axis=2)).astype(jnp.int32)
    source = jnp.arange(EXPERTS, dtype=jnp.int32)[:, None]
    column = (source * MOST + slot_index).astype(jnp.int32)
    row_id = (source * ROWS + jnp.arange(ROWS * TOP, dtype=jnp.int32)[None, :] // TOP).astype(jnp.int32)
    table = jnp.zeros((EXPERTS, EXPERTS * MOST), jnp.int32).at[expert_of, column].set(row_id)
    weight_table = jnp.zeros((EXPERTS, EXPERTS * MOST), jnp.float32).at[expert_of, column].set(weights.reshape(EXPERTS, ROWS * TOP))
    flat_in = moe_in.reshape(EXPERTS * ROWS, model_width)

    def expert_step(running, stacked):
        index_row, weight_row, gate_weight, up_weight, down_weight = stacked
        produced = expert_rows(flat_in[index_row], gate_weight, up_weight, down_weight)
        return (running.at[index_row].add(weight_row[:, None] * produced.astype(jnp.float32)), None)
    moe_out, unused = lax.scan(expert_step, jnp.zeros((EXPERTS * ROWS, model_width), jnp.float32), (table, weight_table, exp_gate, exp_up, exp_down))
    layer_out = residual.reshape(EXPERTS * ROWS, model_width) + moe_out
    return layer_out.reshape(N_SEQ, SEQS * LEN_DEV, model_width)
```

```python
import jax
import jax.numpy as jnp
from jax import lax
from jax.experimental import pallas as pl
from jax.experimental.pallas import tpu as pltpu
from jax.sharding import PartitionSpec as P

DH = 128
BLOCK = 256


epsilon = 1e-06


def laid_out(pieces, dim):
    pieces = jnp.moveaxis(pieces, 0, dim)
    dims = pieces.shape
    return pieces.reshape(*dims[:dim], dims[dim] * dims[dim + 1], *dims[dim + 2 :])


def from_everyone(value, axis):
    copies = jnp.broadcast_to(value, (lax.axis_size(axis), *value.shape))
    return lax.all_to_all(copies, axis, split_axis=0, concat_axis=0, tiled=True)


def gather_directly(value, axis, dim):
    return laid_out(from_everyone(value, axis), dim)


def split_up(value, dim, devices):
    before, after = (value.shape[:dim], value.shape[dim + 1 :])
    return jnp.moveaxis(value.reshape(*before, devices, -1, *after), dim, 0)


def summed_on_arrival(value, axis, dim):
    pieces = split_up(value, dim, lax.axis_size(axis))
    arrived = lax.all_to_all(pieces, axis, split_axis=0, concat_axis=0, tiled=True)
    return arrived.astype(jnp.float32).sum(axis=0)


def rms_scale(values, gain_vec):
    mean_sq = jnp.mean(values * values, axis=-1, keepdims=True)
    return values * lax.rsqrt(mean_sq + epsilon) * gain_vec


MESH = pl.DeviceIdType.MESH
SEQ = 8
HEAD = 16
DEVS = SEQ * HEAD
ROWS = 32
TOP = 8
SLOTS = 3
WIDTH = 2048
HIDDEN = 768
TILES = WIDTH // 128
CHUNK = SLOTS * TILES
HALF = DEVS // 2


def moe_kernel(
    residual_ref,
    gain_ref,
    router_ref,
    picks_ref,
    picks_t_ref,
    gate_hbm,
    up_hbm,
    down_hbm,
    out_ref,
    gate_w,
    up_w,
    down_w,
    spread,
    outgoing,
    arrived,
    result,
    returned,
    rows,
    weight_sem,
    out_sem,
    in_sem,
    back_out_sem,
    back_in_sem,
):
    my_seq = lax.axis_index("seq")
    my_head = lax.axis_index("head")
    me = my_seq * HEAD + my_head
    loads = [
        pltpu.make_async_copy(hbm, vmem, weight_sem.at[i])
        for i, (hbm, vmem) in enumerate(((gate_hbm, gate_w), (up_hbm, up_w), (down_hbm, down_w)))
    ]
    for load in loads:
        load.start()

    barrier = pltpu.get_barrier_semaphore()

    def greet(i, carry):
        other = lax.rem(me + i, DEVS)
        pl.semaphore_signal(
            barrier, inc=1, device_id=(other // HEAD, lax.rem(other, HEAD)), device_id_type=MESH
        )
        return carry

    lax.fori_loop(1, DEVS, greet, 0)

    residual = residual_ref[...]
    moe_in = rms_scale(residual, gain_ref[...]).astype(jnp.bfloat16)
    logits = jnp.dot(moe_in, router_ref[...], preferred_element_type=jnp.float32)
    picks = picks_ref[...]
    picks_t = picks_t_ref[...]
    lane = lax.broadcasted_iota(jnp.int32, (ROWS, DEVS), 1)
    line = lax.broadcasted_iota(jnp.int32, (DEVS, ROWS), 0)
    match = jnp.zeros((ROWS, DEVS), jnp.float32)
    match_t = jnp.zeros((DEVS, ROWS), jnp.float32)
    for k in range(TOP):
        match = match + jnp.where(picks[:, k : k + 1] == lane, 1.0, 0.0)
        match_t = match_t + jnp.where(picks_t[k : k + 1, :] == line, 1.0, 0.0)
    row_i = lax.broadcasted_iota(jnp.int32, (ROWS, ROWS), 0)
    col_i = lax.broadcasted_iota(jnp.int32, (ROWS, ROWS), 1)
    earlier = jnp.where(col_i < row_i, 1.0, 0.0).astype(jnp.bfloat16)
    earlier_t = jnp.where(row_i < col_i, 1.0, 0.0).astype(jnp.bfloat16)
    before = jnp.dot(earlier, match.astype(jnp.bfloat16), preferred_element_type=jnp.float32)
    before_t = jnp.dot(match_t.astype(jnp.bfloat16), earlier_t, preferred_element_type=jnp.float32)
    scores = match * jax.nn.sigmoid(logits)
    weights = scores / jnp.sum(scores, axis=1, keepdims=True)
    select = jnp.concatenate(
        [jnp.where(before_t == float(c), match_t, 0.0) for c in range(SLOTS)], axis=0
    ).astype(jnp.bfloat16)
    for j in range(0, TILES, 2):
        picked = jnp.dot(
            select, moe_in[:, j * 128 : (j + 2) * 128], preferred_element_type=jnp.float32
        )
        for c in range(SLOTS):
            for half in range(2):
                spread[pl.ds(c * TILES + j + half, DEVS, CHUNK), :] = picked[
                    c * DEVS : (c + 1) * DEVS, half * 128 : (half + 1) * 128
                ]
    pl.semaphore_wait(barrier, DEVS - 1)

    for o in range(SEQ):
        to_seq = lax.rem(my_seq + o, SEQ)
        part = pl.multiple_of(to_seq * (HEAD * CHUNK), HEAD * CHUNK)
        outgoing[pl.ds(to_seq * HEAD, HEAD)] = (
            spread[pl.ds(part, HEAD * CHUNK), :].astype(jnp.bfloat16).reshape(HEAD, CHUNK, 128)
        )

        def send(i, carry):
            to_head = lax.rem(my_head + i, HEAD)
            pltpu.make_async_remote_copy(
                src_ref=outgoing.at[to_seq * HEAD + to_head],
                dst_ref=arrived.at[o * HEAD + my_head],
                send_sem=out_sem,
                recv_sem=in_sem.at[o],
                device_id=(to_seq, to_head),
                device_id_type=MESH,
            ).start()
            return carry

        if o == 0:
            pltpu.make_async_copy(
                outgoing.at[me], arrived.at[my_head], in_sem.at[0]
            ).start()
        lax.fori_loop(1 if o == 0 else 0, HEAD, send, 0)

    for load in loads:
        load.wait()
    part_rows = HALF * SLOTS
    for part in range(2):
        for o in range(part * SEQ // 2, (part + 1) * SEQ // 2):
            group = arrived.at[pl.ds(o * HEAD, HEAD)]
            pltpu.make_async_copy(group, group, in_sem.at[o]).wait()
        for q in range(4):
            block = arrived[pl.ds(part * HALF + q * HEAD, HEAD)]
            spread[pl.ds(q * HEAD * CHUNK, HEAD * CHUNK), :] = block.astype(jnp.float32).reshape(
                HEAD * CHUNK, 128
            )
        for j in range(TILES):
            rows[0:part_rows, j * 128 : (j + 1) * 128] = spread[
                pl.ds(j, part_rows, TILES), :
            ].astype(jnp.bfloat16)
        inputs = rows[0:part_rows, :]
        gate_act = jnp.dot(inputs, gate_w[...], preferred_element_type=jnp.float32)
        up_act = jnp.dot(inputs, up_w[...], preferred_element_type=jnp.float32)
        hidden = (jax.nn.silu(gate_act) * up_act).astype(jnp.bfloat16)
        for j in range(0, TILES, 2):
            produced = jnp.dot(
                hidden, down_w[:, j * 128 : (j + 2) * 128], preferred_element_type=jnp.float32
            )
            for half in range(2):
                spread[pl.ds(j + half, part_rows, TILES), :] = produced[
                    :, half * 128 : (half + 1) * 128
                ]
        for o in range(part * SEQ // 2, (part + 1) * SEQ // 2):
            q = o - part * SEQ // 2
            result[pl.ds(o * HEAD, HEAD)] = (
                spread[pl.ds(q * HEAD * CHUNK, HEAD * CHUNK), :]
                .astype(jnp.bfloat16)
                .reshape(HEAD, CHUNK, 128)
            )
            to_seq = lax.rem(my_seq + SEQ - o, SEQ)

            def send_back(i, carry):
                to_head = lax.rem(my_head + i, HEAD)
                pltpu.make_async_remote_copy(
                    src_ref=result.at[o * HEAD + to_head],
                    dst_ref=returned.at[me],
                    send_sem=back_out_sem,
                    recv_sem=back_in_sem,
                    device_id=(to_seq, to_head),
                    device_id_type=MESH,
                ).start()
                return carry

            if o == 0:
                pltpu.make_async_copy(
                    result.at[my_head], returned.at[me], back_in_sem
                ).start()
            lax.fori_loop(1 if o == 0 else 0, HEAD, send_back, 0)

    pltpu.make_async_copy(returned, returned, back_in_sem).wait()
    for q in range(SEQ):
        spread[pl.ds(q * HEAD * CHUNK, HEAD * CHUNK), :] = (
            returned[pl.ds(q * HEAD, HEAD)].astype(jnp.float32).reshape(HEAD * CHUNK, 128)
        )
    for c in range(SLOTS):
        for j in range(TILES):
            rows[c * DEVS : (c + 1) * DEVS, j * 128 : (j + 1) * 128] = spread[
                pl.ds(c * TILES + j, DEVS, CHUNK), :
            ].astype(jnp.bfloat16)
    spread_weights = jnp.concatenate(
        [jnp.where(before == float(c), weights, 0.0) for c in range(SLOTS)], axis=1
    )
    high = spread_weights.astype(jnp.bfloat16)
    low = (spread_weights - high.astype(jnp.float32)).astype(jnp.bfloat16)
    both = jnp.dot(
        jnp.concatenate([high, low], axis=0), rows[...], preferred_element_type=jnp.float32
    )
    out_ref[...] = both[:ROWS] + both[ROWS:]
    sent = outgoing.at[pl.ds(0, DEVS - 1)]
    pltpu.make_async_copy(sent, sent, out_sem).wait()
    sent_back = result.at[pl.ds(0, DEVS - 1)]
    pltpu.make_async_copy(sent_back, sent_back, back_out_sem).wait()


def moe(residual, gain, router, picks, gate_weight, up_weight, down_weight):
    vmem = pl.BlockSpec(memory_space=pltpu.VMEM)
    anywhere = pl.BlockSpec(memory_space=pl.ANY)
    chunks = pltpu.VMEM((DEVS, CHUNK, 128), jnp.bfloat16)
    return pl.pallas_call(
        moe_kernel,
        out_shape=jax.ShapeDtypeStruct((ROWS, WIDTH), jnp.float32),
        in_specs=[vmem] * 5 + [anywhere] * 3,
        out_specs=vmem,
        scratch_shapes=[
            pltpu.VMEM((WIDTH, HIDDEN), jnp.bfloat16),
            pltpu.VMEM((WIDTH, HIDDEN), jnp.bfloat16),
            pltpu.VMEM((HIDDEN, WIDTH), jnp.bfloat16),
            pltpu.VMEM((DEVS * CHUNK, 128), jnp.float32),
            chunks,
            chunks,
            chunks,
            chunks,
            pltpu.VMEM((DEVS * SLOTS, WIDTH), jnp.bfloat16),
            pltpu.SemaphoreType.DMA((3,)),
            pltpu.SemaphoreType.DMA,
            pltpu.SemaphoreType.DMA((SEQ,)),
            pltpu.SemaphoreType.DMA,
            pltpu.SemaphoreType.DMA,
        ],
        compiler_params=pltpu.CompilerParams(
            collective_id=1, has_side_effects=True, vmem_limit_bytes=48 * 1024 * 1024
        ),
        cost_estimate=pl.CostEstimate(
            flops=6 * DEVS * SLOTS * WIDTH * HIDDEN, bytes_accessed=10 << 20, transcendentals=0
        ),
    )(residual, gain, router, picks, picks.T, gate_weight, up_weight, down_weight)


def local(
    tokens,
    attn_gain,
    w_query,
    w_key,
    w_value,
    w_gate,
    head_gain,
    w_out,
    moe_gain,
    w_router,
    expert_picks,
    exp_gate,
    exp_up,
    exp_down,
):
    gathered = gather_directly(tokens, "head", 2)
    seq_count, length, model_width = gathered.shape
    flat_tokens = gathered.reshape(seq_count * length, model_width)
    normed = rms_scale(flat_tokens.astype(jnp.float32), attn_gain).astype(jnp.bfloat16)
    head_width = w_query.shape[1]
    heads_here = head_width // DH
    block_count = length // BLOCK

    def project(weight):
        return jnp.dot(normed, weight, preferred_element_type=jnp.float32)

    block_shape = (seq_count, block_count, BLOCK, heads_here, DH)
    query_blocks = jax.nn.silu(project(w_query)).astype(jnp.bfloat16).reshape(block_shape)
    key_blocks = jax.nn.silu(project(w_key)).astype(jnp.bfloat16).reshape(block_shape)
    value_blocks = jax.nn.silu(project(w_value)).astype(jnp.bfloat16).reshape(block_shape)
    gate_out = jax.nn.sigmoid(project(w_gate))
    causal = jnp.arange(BLOCK)[:, None] >= jnp.arange(BLOCK)[None, :]
    scores = jnp.einsum(
        "snihd,snjhd->snhij", query_blocks, key_blocks, preferred_element_type=jnp.float32
    )
    scores = jnp.where(causal, scores, 0.0).astype(jnp.bfloat16)
    inner_part = jnp.einsum(
        "snhij,snjhd->snihd", scores, value_blocks, preferred_element_type=jnp.float32
    )
    block_states = jnp.einsum(
        "snjhd,snjhe->snhde", key_blocks, value_blocks, preferred_element_type=jnp.float32
    )
    local_total = jnp.sum(block_states, axis=1)
    own_index = lax.axis_index("seq")
    shards = gather_directly(local_total[None].astype(jnp.bfloat16), "seq", 0).astype(jnp.float32)
    owners = jnp.arange(shards.shape[0], dtype=jnp.int32)
    keep_mask = (owners < own_index)[:, None, None, None, None]
    carried = jnp.zeros_like(local_total) + jnp.sum(jnp.where(keep_mask, shards, 0.0), axis=0)
    within = jnp.cumsum(block_states, axis=1) - block_states
    prefix = (carried[:, None] + within).astype(jnp.bfloat16)
    outer_part = jnp.einsum(
        "snihd,snhde->snihe", query_blocks, prefix, preferred_element_type=jnp.float32
    )
    mixed = (inner_part + outer_part).reshape(seq_count * length, heads_here, DH)
    normed_heads = rms_scale(mixed, head_gain.reshape(heads_here, DH))
    gated_out = (normed_heads.reshape(seq_count * length, head_width) * gate_out).astype(
        jnp.bfloat16
    )
    row_count = expert_picks.shape[1]
    attn_rows = summed_on_arrival(
        jnp.dot(gated_out, w_out, preferred_element_type=jnp.float32).astype(jnp.bfloat16),
        "head",
        0,
    )
    first_row = lax.axis_index("head") * row_count
    residual = (
        lax.dynamic_slice_in_dim(flat_tokens, first_row, row_count, 0).astype(jnp.float32)
        + attn_rows
    )
    moe_out = moe(
        residual,
        moe_gain[None],
        w_router,
        expert_picks[0],
        exp_gate[0],
        exp_up[0],
        exp_down[0],
    )
    return (residual + moe_out)[None]


def solution(mesh):
    placed = (
        P(None, "seq", "head"),
        P(),
        P(None, "head"),
        P(None, "head"),
        P(None, "head"),
        P(None, "head"),
        P("head"),
        P("head", None),
        P(),
        P(),
        P("seq", "head", None),
        P(("seq", "head"), None, None),
        P(("seq", "head"), None, None),
        P(("seq", "head"), None, None),
    )
    return jax.shard_map(
        local, mesh=mesh, in_specs=placed, out_specs=P("seq", "head", None), check_vma=False
    )
```

```python
import jax
import jax.numpy as jnp
from jax import lax
from jax.experimental import pallas as pl
from jax.experimental.pallas import tpu as pltpu
from jax.sharding import PartitionSpec as P

MESH = pl.DeviceIdType.MESH
SEQ = 8
HEAD = 16
DEVS = SEQ * HEAD
DH = 128
BLOCK = 256
ROWS = 32
TOP = 8
SLOTS = 3
WIDTH = 2048
HIDDEN = 768
TILES = WIDTH // 128
CHUNK = SLOTS * TILES
HALF = DEVS // 2
HERE = 256
WIDE = WIDTH // 2
PIECE = WIDE // 2
FAR_FIRST = (2, 3, 1, 0)

epsilon = 1e-06


def rms_scale(values, gain_vec):
    mean_sq = jnp.mean(values * values, axis=-1, keepdims=True)
    return values * lax.rsqrt(mean_sq + epsilon) * gain_vec


def dot(a, b):
    return jnp.dot(a, b, preferred_element_type=jnp.float32)


def arrived_in(ref, sem):
    pltpu.make_async_copy(ref, ref, sem).wait()


def layer_kernel(
    tokens_hbm,
    attn_gain_hbm,
    query_hbm,
    key_hbm,
    value_hbm,
    gate_hbm,
    head_gain_hbm,
    out_hbm,
    moe_gain_hbm,
    router_hbm,
    picks_hbm,
    exp_gate_hbm,
    exp_up_hbm,
    exp_down_hbm,
    layer_out,
    attn_gain,
    w_query,
    w_key,
    w_value,
    w_gate,
    head_gain,
    w_out,
    moe_gain,
    w_router,
    picks_ref,
    gate_w,
    up_w,
    down_w,
    gathered,
    squares,
    acc,
    keys,
    values,
    states,
    pair_out,
    pair_in,
    total_out,
    total_in,
    prefix_out,
    prefix_in,
    mixed,
    gated,
    partial,
    near_sum,
    s1,
    r1,
    s2,
    r2,
    s3,
    r3,
    s4,
    r4,
    select,
    match_ref,
    before_ref,
    residual_ref,
    spread,
    outgoing,
    arrived,
    result,
    returned,
    rows,
    load_sem,
    own_sem,
    gather_out,
    first_in,
    second_in,
    state_out,
    state_in,
    sum_out,
    sum1_in,
    sum2_in,
    sum3_in,
    sum4_in,
    out_sem,
    in_sem,
    back_out_sem,
    back_in_sem,
):
    my_seq = lax.axis_index("seq")
    my_head = lax.axis_index("head")
    me = my_seq * HEAD + my_head
    my_x = lax.rem(my_head, 4)
    my_y = my_head // 4
    my_z = my_seq // 2
    my_core = lax.rem(my_seq, 2)
    other_core = my_seq + 1 - 2 * my_core

    def head_at(t, first, second):
        dx, dy = (first, second) if t == 0 else (second, first)
        return lax.rem(my_y + dy, 4) * 4 + lax.rem(my_x + dx, 4)

    barrier = pltpu.get_barrier_semaphore()
    partners = [(my_seq, head_at(0, 1, 0)), (my_seq, head_at(0, 3, 0))]
    partners += [(my_seq, head_at(0, 0, 1)), (my_seq, head_at(0, 0, 3))]
    partners += [(other_core, my_head)]
    partners += [(lax.rem(my_z + dz, 4) * 2 + my_core, my_head) for dz in (1, 2, 3)]
    for partner in partners:
        pl.semaphore_signal(barrier, inc=1, device_id=partner, device_id_type=MESH)
    own = pltpu.make_async_copy(tokens_hbm, gathered.at[my_head], own_sem)
    own.start()
    loads = [
        pltpu.make_async_copy(hbm, vmem, load_sem.at[i])
        for i, (hbm, vmem) in enumerate(
            (
                (attn_gain_hbm, attn_gain),
                (query_hbm, w_query),
                (key_hbm, w_key),
                (value_hbm, w_value),
                (gate_hbm, w_gate),
                (picks_hbm, picks_ref),
                (head_gain_hbm, head_gain),
                (out_hbm, w_out),
                (moe_gain_hbm, moe_gain),
                (router_hbm, w_router),
                (exp_gate_hbm, gate_w),
                (exp_up_hbm, up_w),
                (exp_down_hbm, down_w),
            )
        )
    ]
    for load in loads:
        load.start()
    pl.semaphore_wait(barrier, len(partners))

    def push(source, target, t, first, second, send_sem, recv_sem):
        pltpu.make_async_remote_copy(
            src_ref=source,
            dst_ref=target,
            send_sem=send_sem,
            recv_sem=recv_sem,
            device_id=(my_seq, head_at(t, first, second)),
            device_id_type=MESH,
        ).start()

    def block(t, first, second):
        return gathered.at[head_at(t, first, second), t]

    def part(ref, i):
        return ref.at[pl.ds(i * BLOCK // 2, BLOCK // 2)]

    def pass_on(t, first, source):
        here = block(t, first, 0)
        push(source, here, t, 0, 1, gather_out, second_in.at[t, first, 0])
        push(source, here, t, 0, 3, gather_out, second_in.at[t, first, 1])

    for t in range(2):
        mine = block(t, 0, 0)
        push(tokens_hbm.at[t], mine, t, 1, 0, gather_out, first_in.at[t, 0])
        push(tokens_hbm.at[t], mine, t, 3, 0, gather_out, first_in.at[t, 1])
        pass_on(t, 0, tokens_hbm.at[t])

    loads[5].wait()
    picks = picks_ref[0]
    lane = lax.broadcasted_iota(jnp.int32, (ROWS, DEVS), 1)
    match = jnp.zeros((ROWS, DEVS), jnp.float32)
    for k in range(TOP):
        match = match + jnp.where(picks[:, k : k + 1] == lane, 1.0, 0.0)
    row_i = lax.broadcasted_iota(jnp.int32, (ROWS, ROWS), 0)
    col_i = lax.broadcasted_iota(jnp.int32, (ROWS, ROWS), 1)
    earlier = jnp.where(col_i < row_i, 1.0, 0.0).astype(jnp.bfloat16)
    before = dot(earlier, match.astype(jnp.bfloat16))
    match_ref[...] = match
    before_ref[...] = before
    for c in range(SLOTS):
        select[c * DEVS : (c + 1) * DEVS, :] = jnp.transpose(
            jnp.where(before == float(c), match, 0.0)
        ).astype(jnp.bfloat16)

    for t in range(2):
        arrived_in(block(t, 3, 0), first_in.at[t, 0])
        push(part(block(t, 3, 0), 0), part(block(t, 3, 0), 0), t, 1, 0, gather_out, first_in.at[t, 2])
        pass_on(t, 3, block(t, 3, 0))
        arrived_in(block(t, 1, 0), first_in.at[t, 1])
        push(part(block(t, 1, 0), 1), part(block(t, 1, 0), 1), t, 3, 0, gather_out, first_in.at[t, 3])
        pass_on(t, 1, block(t, 1, 0))
    for t in range(2):
        arrived_in(part(block(t, 2, 0), 0), first_in.at[t, 2])
        arrived_in(part(block(t, 2, 0), 1), first_in.at[t, 3])
        pass_on(t, 2, block(t, 2, 0))

    own.wait()
    for i in range(5):
        loads[i].wait()
    weights_in = (w_query, w_key, w_value, w_gate)

    def project_line(t, second):
        heads = [head_at(t, first, second) for first in range(4)]
        total = None
        pieces = []
        for h in heads:
            piece = gathered[h, t].astype(jnp.float32)
            square = piece * piece
            total = square if total is None else total + square
            pieces.append((piece * attn_gain[pl.ds(h, 1), :]).astype(jnp.bfloat16))
        if second == 0:
            squares[t] = total
        else:
            squares[t] += total
        line = jnp.concatenate(pieces, axis=1)
        for i, weight in enumerate(weights_in):
            deep = jnp.concatenate(
                [weight[pl.ds(pl.multiple_of(h * 128, 128), 128), :] for h in heads], axis=0
            )
            product = dot(line, deep)
            if second == 0:
                acc[t, :, i * HERE : (i + 1) * HERE] = product
            else:
                acc[t, :, i * HERE : (i + 1) * HERE] += product

    def forward_line(t):
        for first in (0, 3, 1, 2):
            lower = block(t, first, 3)
            arrived_in(lower, second_in.at[t, first, 0])
            push(part(lower, 0), part(lower, 0), t, 0, 1, gather_out, second_in.at[t, first, 2])
            upper = block(t, first, 1)
            arrived_in(upper, second_in.at[t, first, 1])
            push(part(upper, 1), part(upper, 1), t, 0, 3, gather_out, second_in.at[t, first, 3])

    project_line(0, 0)
    project_line(1, 0)
    forward_line(0)
    forward_line(1)
    for t in range(2):
        project_line(t, 3)
        project_line(t, 1)
    for t in range(2):
        for first in (0, 3, 1, 2):
            arrived_in(part(block(t, first, 2), 0), second_in.at[t, first, 2])
            arrived_in(part(block(t, first, 2), 1), second_in.at[t, first, 3])
        project_line(t, 2)

    def scale_of(t):
        mean_sq = jnp.sum(squares[t], axis=-1, keepdims=True) * (1.0 / WIDTH)
        return lax.rsqrt(mean_sq + epsilon)

    for t in range(2):
        scale = scale_of(t)
        keys[t] = jax.nn.silu(acc[t, :, HERE : 2 * HERE] * scale).astype(jnp.bfloat16)
        values[t] = jax.nn.silu(acc[t, :, 2 * HERE : 3 * HERE] * scale).astype(jnp.bfloat16)
        for h in range(2):
            states[t, h] = lax.dot_general(
                keys[t, :, h * DH : (h + 1) * DH],
                values[t, :, h * DH : (h + 1) * DH],
                (((0,), (0,)), ((), ())),
                preferred_element_type=jnp.float32,
            )
    pair_out[...] = states[1 - my_core].astype(jnp.bfloat16)
    pair = pltpu.make_async_remote_copy(
        src_ref=pair_out,
        dst_ref=pair_in,
        send_sem=state_out.at[0],
        recv_sem=state_in.at[0],
        device_id=(other_core, my_head),
        device_id_type=MESH,
    )
    pair.start()

    causal = lax.broadcasted_iota(jnp.int32, (BLOCK, BLOCK), 0) >= lax.broadcasted_iota(
        jnp.int32, (BLOCK, BLOCK), 1
    )

    def inner(t):
        queries = jax.nn.silu(acc[t, :, 0:HERE] * scale_of(t)).astype(jnp.bfloat16)
        gated[t] = queries
        for h in range(2):
            cols = slice(h * DH, (h + 1) * DH)
            scores = lax.dot_general(
                queries[:, cols],
                keys[t, :, cols],
                (((1,), (1,)), ((), ())),
                preferred_element_type=jnp.float32,
            )
            scores = jnp.where(causal, scores, 0.0).astype(jnp.bfloat16)
            mixed[t, :, cols] = dot(scores, values[t, :, cols])

    pair.wait_recv()
    total_out[...] = (states[my_core] + pair_in[...].astype(jnp.float32)).astype(jnp.bfloat16)
    totals = [
        pltpu.make_async_remote_copy(
            src_ref=total_out,
            dst_ref=total_in.at[dz - 1],
            send_sem=state_out.at[dz],
            recv_sem=state_in.at[dz],
            device_id=(lax.rem(my_z + dz, 4) * 2 + my_core, my_head),
            device_id_type=MESH,
        )
        for dz in (1, 2, 3)
    ]
    for total in totals:
        total.start()
    inner(0)
    inner(1)
    base = jnp.zeros((2, DH, DH), jnp.float32)
    for dz in (1, 2, 3):
        totals[dz - 1].wait_recv()
        earlier_chip = jnp.where(my_z >= dz, 1.0, 0.0)
        base = base + earlier_chip * total_in[dz - 1].astype(jnp.float32)
    second_core = my_core.astype(jnp.float32)
    prefix_out[1] = (base + second_core * pair_in[...].astype(jnp.float32)).astype(jnp.bfloat16)
    prefix_out[0] = (base + (1.0 - second_core) * states[my_core]).astype(jnp.bfloat16)
    hand_over = pltpu.make_async_remote_copy(
        src_ref=prefix_out.at[0],
        dst_ref=prefix_in,
        send_sem=state_out.at[4],
        recv_sem=state_in.at[4],
        device_id=(other_core, my_head),
        device_id_type=MESH,
    )
    hand_over.start()
    for i in (6, 7):
        loads[i].wait()
    hand_over.wait_recv()

    for t in range(2):
        gate = jax.nn.sigmoid(acc[t, :, 3 * HERE : 4 * HERE] * scale_of(t))
        for h in range(2):
            cols = slice(h * DH, (h + 1) * DH)
            prefix = jnp.where(my_core == t, prefix_out[1, h], prefix_in[h])
            whole = mixed[t, :, cols] + dot(gated[t, :, cols], prefix)
            normed = rms_scale(whole, head_gain[h : h + 1, :])
            gated[t, :, cols] = (normed * gate[:, cols]).astype(jnp.bfloat16)
    for t in range(2):
        for j in range(4):
            cols = slice(j * 512, (j + 1) * 512)
            partial[t * BLOCK : (t + 1) * BLOCK, cols] = dot(gated[t], w_out[:, cols])

    def own_part(t, first, second, low, high):
        start = pl.multiple_of(head_at(t, first, second) * ROWS, ROWS)
        return partial[pl.ds(start, ROWS), t * WIDE + low : t * WIDE + high]

    for k in FAR_FIRST:
        for t in range(2):
            s1[t, k, 0] = own_part(t, k, 2, 0, PIECE).astype(jnp.bfloat16)
            push(s1.at[t, k, 0], r1.at[t, k, 0], t, 0, 1, sum_out.at[0], sum1_in.at[t, k, 0])
            s1[t, k, 1] = own_part(t, k, 2, PIECE, WIDE).astype(jnp.bfloat16)
            push(s1.at[t, k, 1], r1.at[t, k, 1], t, 0, 3, sum_out.at[0], sum1_in.at[t, k, 1])
    for k in FAR_FIRST:
        for t in range(2):
            arrived_in(r1.at[t, k, 0], sum1_in.at[t, k, 0])
            s2[t, k, 0, :, 0:PIECE] = (
                own_part(t, k, 1, 0, PIECE) + r1[t, k, 0].astype(jnp.float32)
            ).astype(jnp.bfloat16)
            s2[t, k, 0, :, PIECE:WIDE] = own_part(t, k, 1, PIECE, WIDE).astype(jnp.bfloat16)
            push(s2.at[t, k, 0], r2.at[t, k, 0], t, 0, 1, sum_out.at[1], sum2_in.at[t, k, 0])
            arrived_in(r1.at[t, k, 1], sum1_in.at[t, k, 1])
            s2[t, k, 1, :, 0:PIECE] = own_part(t, k, 3, 0, PIECE).astype(jnp.bfloat16)
            s2[t, k, 1, :, PIECE:WIDE] = (
                own_part(t, k, 3, PIECE, WIDE) + r1[t, k, 1].astype(jnp.float32)
            ).astype(jnp.bfloat16)
            push(s2.at[t, k, 1], r2.at[t, k, 1], t, 0, 3, sum_out.at[1], sum2_in.at[t, k, 1])
    for k in FAR_FIRST:
        for t in range(2):
            arrived_in(r2.at[t, k, 0], sum2_in.at[t, k, 0])
            arrived_in(r2.at[t, k, 1], sum2_in.at[t, k, 1])
            line_sum = (
                own_part(t, k, 0, 0, WIDE)
                + r2[t, k, 0].astype(jnp.float32)
                + r2[t, k, 1].astype(jnp.float32)
            )
            if k == 2:
                s3[t, 0] = line_sum[:, :PIECE].astype(jnp.bfloat16)
                push(s3.at[t, 0], r3.at[t, 0], t, 1, 0, sum_out.at[2], sum3_in.at[t, 0])
                s3[t, 1] = line_sum[:, PIECE:].astype(jnp.bfloat16)
                push(s3.at[t, 1], r3.at[t, 1], t, 3, 0, sum_out.at[2], sum3_in.at[t, 1])
            else:
                near_sum[t, k] = line_sum
    for t in range(2):
        arrived_in(r3.at[t, 0], sum3_in.at[t, 0])
        s4[t, 0, :, 0:PIECE] = (
            near_sum[t, 1, :, 0:PIECE] + r3[t, 0].astype(jnp.float32)
        ).astype(jnp.bfloat16)
        s4[t, 0, :, PIECE:WIDE] = near_sum[t, 1, :, PIECE:WIDE].astype(jnp.bfloat16)
        push(s4.at[t, 0], r4.at[t, 0], t, 1, 0, sum_out.at[3], sum4_in.at[t, 0])
        arrived_in(r3.at[t, 1], sum3_in.at[t, 1])
        s4[t, 1, :, 0:PIECE] = near_sum[t, 3, :, 0:PIECE].astype(jnp.bfloat16)
        s4[t, 1, :, PIECE:WIDE] = (
            near_sum[t, 3, :, PIECE:WIDE] + r3[t, 1].astype(jnp.float32)
        ).astype(jnp.bfloat16)
        push(s4.at[t, 1], r4.at[t, 1], t, 3, 0, sum_out.at[3], sum4_in.at[t, 1])
    own_start = pl.multiple_of(lax.rem(my_head, 8) * ROWS, ROWS)
    for j in range(TILES):
        residual_ref[:, j * 128 : (j + 1) * 128] = gathered[
            j, my_head // 8, pl.ds(own_start, ROWS), :
        ].astype(jnp.float32)
    for t in range(2):
        arrived_in(r4.at[t, 0], sum4_in.at[t, 0])
        arrived_in(r4.at[t, 1], sum4_in.at[t, 1])
        residual_ref[:, t * WIDE : (t + 1) * WIDE] += (
            near_sum[t, 0] + r4[t, 0].astype(jnp.float32) + r4[t, 1].astype(jnp.float32)
        )

    for i in (8, 9):
        loads[i].wait()
    moe_in = rms_scale(residual_ref[...], moe_gain[...]).astype(jnp.bfloat16)
    for j in range(0, TILES, 2):
        picked = dot(select[...], moe_in[:, j * 128 : (j + 2) * 128])
        for c in range(SLOTS):
            for half in range(2):
                spread[pl.ds(c * TILES + j + half, DEVS, CHUNK), :] = picked[
                    c * DEVS : (c + 1) * DEVS, half * 128 : (half + 1) * 128
                ]
    for o in range(SEQ):
        to_seq = lax.rem(my_seq + o, SEQ)
        start = pl.multiple_of(to_seq * (HEAD * CHUNK), HEAD * CHUNK)
        outgoing[pl.ds(to_seq * HEAD, HEAD)] = (
            spread[pl.ds(start, HEAD * CHUNK), :].astype(jnp.bfloat16).reshape(HEAD, CHUNK, 128)
        )

        def send(i, carry):
            to_head = lax.rem(my_head + i, HEAD)
            pltpu.make_async_remote_copy(
                src_ref=outgoing.at[to_seq * HEAD + to_head],
                dst_ref=arrived.at[o * HEAD + my_head],
                send_sem=out_sem,
                recv_sem=in_sem.at[o],
                device_id=(to_seq, to_head),
                device_id_type=MESH,
            ).start()
            return carry

        if o == 0:
            pltpu.make_async_copy(outgoing.at[me], arrived.at[my_head], in_sem.at[0]).start()
        lax.fori_loop(1 if o == 0 else 0, HEAD, send, 0)

    logits = dot(moe_in, w_router[...])
    scores = match_ref[...] * jax.nn.sigmoid(logits)
    weights = scores / jnp.sum(scores, axis=1, keepdims=True)
    before = before_ref[...]
    spread_weights = jnp.concatenate(
        [jnp.where(before == float(c), weights, 0.0) for c in range(SLOTS)], axis=1
    )
    high = spread_weights.astype(jnp.bfloat16)
    low = (spread_weights - high.astype(jnp.float32)).astype(jnp.bfloat16)
    combine = jnp.concatenate([high, low], axis=0)

    for i in (10, 11, 12):
        loads[i].wait()
    part_rows = HALF * SLOTS
    for p in range(2):
        for o in range(p * SEQ // 2, (p + 1) * SEQ // 2):
            group = arrived.at[pl.ds(o * HEAD, HEAD)]
            arrived_in(group, in_sem.at[o])
        for q in range(4):
            chunk = arrived[pl.ds(p * HALF + q * HEAD, HEAD)]
            spread[pl.ds(q * HEAD * CHUNK, HEAD * CHUNK), :] = chunk.astype(jnp.float32).reshape(
                HEAD * CHUNK, 128
            )
        for j in range(TILES):
            rows[0:part_rows, j * 128 : (j + 1) * 128] = spread[
                pl.ds(j, part_rows, TILES), :
            ].astype(jnp.bfloat16)
        inputs = rows[0:part_rows, :]
        hidden = (jax.nn.silu(dot(inputs, gate_w[...])) * dot(inputs, up_w[...])).astype(
            jnp.bfloat16
        )
        for j in range(0, TILES, 2):
            produced = dot(hidden, down_w[:, j * 128 : (j + 2) * 128])
            for half in range(2):
                spread[pl.ds(j + half, part_rows, TILES), :] = produced[
                    :, half * 128 : (half + 1) * 128
                ]
        for o in range(p * SEQ // 2, (p + 1) * SEQ // 2):
            q = o - p * SEQ // 2
            result[pl.ds(o * HEAD, HEAD)] = (
                spread[pl.ds(q * HEAD * CHUNK, HEAD * CHUNK), :]
                .astype(jnp.bfloat16)
                .reshape(HEAD, CHUNK, 128)
            )
            to_seq = lax.rem(my_seq + SEQ - o, SEQ)

            def send_back(i, carry):
                to_head = lax.rem(my_head + i, HEAD)
                pltpu.make_async_remote_copy(
                    src_ref=result.at[o * HEAD + to_head],
                    dst_ref=returned.at[me],
                    send_sem=back_out_sem,
                    recv_sem=back_in_sem,
                    device_id=(to_seq, to_head),
                    device_id_type=MESH,
                ).start()
                return carry

            if o == 0:
                pltpu.make_async_copy(result.at[my_head], returned.at[me], back_in_sem).start()
            lax.fori_loop(1 if o == 0 else 0, HEAD, send_back, 0)

    arrived_in(returned, back_in_sem)
    for q in range(SEQ):
        spread[pl.ds(q * HEAD * CHUNK, HEAD * CHUNK), :] = (
            returned[pl.ds(q * HEAD, HEAD)].astype(jnp.float32).reshape(HEAD * CHUNK, 128)
        )
    for c in range(SLOTS):
        for j in range(TILES):
            rows[c * DEVS : (c + 1) * DEVS, j * 128 : (j + 1) * 128] = spread[
                pl.ds(c * TILES + j, DEVS, CHUNK), :
            ].astype(jnp.bfloat16)
    both = dot(combine, rows[...])
    layer_out[0] = residual_ref[...] + both[:ROWS] + both[ROWS:]

    sent = gathered.at[pl.ds(0, HEAD - 1)]
    pltpu.make_async_copy(sent, sent, gather_out).wait()
    pair.wait_send()
    for total in totals:
        total.wait_send()
    hand_over.wait_send()
    for i, ref in enumerate((s1, s2, s3, s4)):
        pltpu.make_async_copy(ref, ref, sum_out.at[i]).wait()
    sent = outgoing.at[pl.ds(0, DEVS - 1)]
    pltpu.make_async_copy(sent, sent, out_sem).wait()
    sent = result.at[pl.ds(0, DEVS - 1)]
    pltpu.make_async_copy(sent, sent, back_out_sem).wait()


def local(
    tokens,
    attn_gain,
    w_query,
    w_key,
    w_value,
    w_gate,
    head_gain,
    w_out,
    moe_gain,
    w_router,
    expert_picks,
    exp_gate,
    exp_up,
    exp_down,
):
    args = (
        tokens,
        attn_gain.reshape(TILES, 128),
        w_query,
        w_key,
        w_value,
        w_gate,
        head_gain.reshape(2, DH),
        w_out,
        moe_gain.reshape(1, WIDTH),
        w_router,
        expert_picks,
        exp_gate[0],
        exp_up[0],
        exp_down[0],
    )

    def half(*shape):
        return pltpu.VMEM(shape, jnp.bfloat16)

    def full(*shape):
        return pltpu.VMEM(shape, jnp.float32)

    def sems(*shape):
        return pltpu.SemaphoreType.DMA(shape)

    return pl.pallas_call(
        layer_kernel,
        out_shape=jax.ShapeDtypeStruct((1, ROWS, WIDTH), jnp.float32),
        in_specs=[pl.BlockSpec(memory_space=pl.ANY)] * len(args),
        out_specs=pl.BlockSpec(memory_space=pltpu.VMEM),
        scratch_shapes=[pltpu.VMEM(a.shape, a.dtype) for a in args[1:]]
        + [
            half(HEAD, 2, BLOCK, 128),
            full(2, BLOCK, 128),
            full(2, BLOCK, 4 * HERE),
            half(2, BLOCK, HERE),
            half(2, BLOCK, HERE),
            full(2, 2, DH, DH),
            half(2, DH, DH),
            half(2, DH, DH),
            half(2, DH, DH),
            half(3, 2, DH, DH),
            half(2, 2, DH, DH),
            half(2, DH, DH),
            full(2, BLOCK, HERE),
            half(2, BLOCK, HERE),
            full(2 * BLOCK, WIDTH),
            full(2, 4, ROWS, WIDE),
            half(2, 4, 2, ROWS, PIECE),
            half(2, 4, 2, ROWS, PIECE),
            half(2, 4, 2, ROWS, WIDE),
            half(2, 4, 2, ROWS, WIDE),
            half(2, 2, ROWS, PIECE),
            half(2, 2, ROWS, PIECE),
            half(2, 2, ROWS, WIDE),
            half(2, 2, ROWS, WIDE),
            half(DEVS * SLOTS, ROWS),
            full(ROWS, DEVS),
            full(ROWS, DEVS),
            full(ROWS, WIDTH),
            full(DEVS * CHUNK, 128),
            half(DEVS, CHUNK, 128),
            half(DEVS, CHUNK, 128),
            half(DEVS, CHUNK, 128),
            half(DEVS, CHUNK, 128),
            half(DEVS * SLOTS, WIDTH),
            sems(13),
            sems(),
            sems(),
            sems(2, 4),
            sems(2, 4, 4),
            sems(5),
            sems(5),
            sems(4),
            sems(2, 4, 2),
            sems(2, 4, 2),
            sems(2, 2),
            sems(2, 2),
            sems(),
            sems(SEQ),
            sems(),
            sems(),
        ],
        compiler_params=pltpu.CompilerParams(
            collective_id=1, has_side_effects=True, vmem_limit_bytes=56 * 1024 * 1024
        ),
        cost_estimate=pl.CostEstimate(
            flops=7 << 30, bytes_accessed=20 << 20, transcendentals=0
        ),
    )(*args)


def solution(mesh):
    placed = (
        P(None, "seq", "head"),
        P(),
        P(None, "head"),
        P(None, "head"),
        P(None, "head"),
        P(None, "head"),
        P("head"),
        P("head", None),
        P(),
        P(),
        P("seq", "head", None),
        P(("seq", "head"), None, None),
        P(("seq", "head"), None, None),
        P(("seq", "head"), None, None),
    )
    return jax.shard_map(
        local, mesh=mesh, in_specs=placed, out_specs=P("seq", "head", None), check_vma=False
    )
```

```python
import jax
import jax.numpy as jnp
from jax import lax
from jax.experimental import pallas as pl
from jax.experimental.pallas import tpu as pltpu
from jax.sharding import PartitionSpec as P

MESH = pl.DeviceIdType.MESH
SEQ = 8
HEAD = 16
DEVS = SEQ * HEAD
DH = 128
BLOCK = 256
ROWS = 32
TOP = 8
SLOTS = 3
WIDTH = 2048
HIDDEN = 768
TILES = WIDTH // 128
CHUNK = SLOTS * TILES
GROUPS = 4
MEMBERS = DEVS // GROUPS
HERE = 256
WIDE = WIDTH // 2
PIECE = WIDE // 2
FAR_FIRST = (2, 3, 1, 0)

epsilon = 1e-06


def rms_scale(values, gain_vec):
    mean_sq = jnp.mean(values * values, axis=-1, keepdims=True)
    return values * lax.rsqrt(mean_sq + epsilon) * gain_vec


def dot(a, b):
    return jnp.dot(a, b, preferred_element_type=jnp.float32)


def arrived_in(ref, sem):
    pltpu.make_async_copy(ref, ref, sem).wait()


def layer_kernel(
    tokens_hbm,
    attn_gain_hbm,
    query_hbm,
    key_hbm,
    value_hbm,
    gate_hbm,
    head_gain_hbm,
    out_hbm,
    moe_gain_hbm,
    router_hbm,
    picks_hbm,
    exp_gate_hbm,
    exp_up_hbm,
    exp_down_hbm,
    residual_ref,
    moe_ref,
    attn_gain,
    w_query,
    w_key,
    w_value,
    w_gate,
    head_gain,
    w_out,
    moe_gain,
    w_router,
    picks_ref,
    gate_w,
    up_w,
    down_w,
    gathered,
    squares,
    acc,
    keys,
    values,
    states,
    pair_out,
    pair_in,
    total_out,
    total_in,
    prefix_out,
    prefix_in,
    mixed,
    gated,
    partial,
    near_sum,
    s1,
    r1,
    s2,
    r2,
    s3,
    r3,
    select,
    match_ref,
    permute,
    slot_ref,
    spread,
    outgoing,
    arrived,
    result,
    returned,
    rows,
    load_sem,
    own_sem,
    gather_out,
    first_in,
    second_in,
    state_out,
    state_in,
    sum_out,
    sum1_in,
    sum2_in,
    sum3_in,
    out_sem,
    in_sem,
    back_out_sem,
    back_in_sem,
):
    my_seq = lax.axis_index("seq")
    my_head = lax.axis_index("head")
    me = my_seq * HEAD + my_head
    my_x = lax.rem(my_head, 4)
    my_y = my_head // 4
    my_z = my_seq // 2
    my_core = lax.rem(my_seq, 2)
    other_core = my_seq + 1 - 2 * my_core

    def head_at(t, first, second):
        dx, dy = (first, second) if t == 0 else (second, first)
        return lax.rem(my_y + dy, 4) * 4 + lax.rem(my_x + dx, 4)

    barrier = pltpu.get_barrier_semaphore()
    partners = [(my_seq, head_at(0, 1, 0)), (my_seq, head_at(0, 3, 0))]
    partners += [(my_seq, head_at(0, 0, 1)), (my_seq, head_at(0, 0, 3))]
    partners += [(my_seq, head_at(0, 2, 0)), (my_seq, head_at(0, 0, 2))]
    partners += [(other_core, my_head)]
    partners += [(lax.rem(my_z + dz, 4) * 2 + my_core, my_head) for dz in (1, 2, 3)]
    for partner in partners:
        pl.semaphore_signal(barrier, inc=1, device_id=partner, device_id_type=MESH)
    own = pltpu.make_async_copy(tokens_hbm, gathered.at[my_head], own_sem)
    own.start()
    loads = [
        pltpu.make_async_copy(hbm, vmem, load_sem.at[i])
        for i, (hbm, vmem) in enumerate(
            (
                (attn_gain_hbm, attn_gain),
                (query_hbm, w_query),
                (key_hbm, w_key),
                (value_hbm, w_value),
                (gate_hbm, w_gate),
                (picks_hbm, picks_ref),
                (head_gain_hbm, head_gain),
                (out_hbm, w_out),
                (moe_gain_hbm, moe_gain),
                (router_hbm, w_router),
                (exp_gate_hbm, gate_w),
                (exp_up_hbm, up_w),
                (exp_down_hbm, down_w),
            )
        )
    ]
    for load in loads:
        load.start()
    pl.semaphore_wait(barrier, len(partners))

    def push(source, target, t, first, second, send_sem, recv_sem):
        pltpu.make_async_remote_copy(
            src_ref=source,
            dst_ref=target,
            send_sem=send_sem,
            recv_sem=recv_sem,
            device_id=(my_seq, head_at(t, first, second)),
            device_id_type=MESH,
        ).start()

    def block(t, first, second):
        return gathered.at[head_at(t, first, second), t]

    def part(ref, i):
        return ref.at[pl.ds(i * BLOCK // 2, BLOCK // 2)]

    def pass_on(t, first, source):
        here = block(t, first, 0)
        push(source, here, t, 0, 1, gather_out, second_in.at[t, first, 0])
        push(source, here, t, 0, 3, gather_out, second_in.at[t, first, 1])

    for t in range(2):
        for step in (1, 3, 2):
            push(tokens_hbm.at[t], block(t, 0, 0), t, step, 0, gather_out, first_in.at[t, 4 - step])
    for t in range(2):
        pass_on(t, 0, tokens_hbm.at[t])

    loads[5].wait()
    line = lax.broadcasted_iota(jnp.int32, (DEVS, ROWS), 0)
    offset = line // MEMBERS
    step_x = lax.rem(line, 4)
    expert_x = lax.rem(my_x + step_x, 4)
    expert_y = lax.rem(my_y + step_x + offset, 4)
    expert_seq = lax.rem(my_seq + lax.rem(line // 4, SEQ), SEQ)
    expert = expert_seq * HEAD + expert_y * 4 + expert_x
    picks = picks_ref[0]
    match_t = jnp.zeros((DEVS, ROWS), jnp.float32)
    near_t = jnp.zeros((DEVS, ROWS), jnp.float32)
    for k in range(TOP):
        match_t = match_t + jnp.where(picks[k : k + 1, :] == line, 1.0, 0.0)
        near_t = near_t + jnp.where(picks[k : k + 1, :] == expert, 1.0, 0.0)
    row_i = lax.broadcasted_iota(jnp.int32, (ROWS, ROWS), 0)
    col_i = lax.broadcasted_iota(jnp.int32, (ROWS, ROWS), 1)
    earlier_t = jnp.where(row_i < col_i, 1.0, 0.0).astype(jnp.bfloat16)
    before_t = dot(near_t.astype(jnp.bfloat16), earlier_t)
    match_ref[...] = jnp.transpose(match_t)
    slot_ref[...] = jnp.where(near_t > 0.0, before_t, float(SLOTS))
    all_lanes = lax.broadcasted_iota(jnp.int32, (DEVS, DEVS), 1)
    permute[...] = jnp.where(expert[:, 0:1] == all_lanes, 1.0, 0.0).astype(jnp.bfloat16)
    for c in range(SLOTS):
        select[c * DEVS : (c + 1) * DEVS, :] = jnp.where(before_t == float(c), near_t, 0.0).astype(
            jnp.bfloat16
        )

    for first in (3, 1, 2):
        for t in range(2):
            arrived_in(block(t, first, 0), first_in.at[t, first])
            pass_on(t, first, block(t, first, 0))

    def forward_line(first):
        for t in range(2):
            lower = block(t, first, 3)
            arrived_in(lower, second_in.at[t, first, 0])
            push(part(lower, 0), part(lower, 0), t, 0, 1, gather_out, second_in.at[t, first, 2])
            upper = block(t, first, 1)
            arrived_in(upper, second_in.at[t, first, 1])
            push(part(upper, 1), part(upper, 1), t, 0, 3, gather_out, second_in.at[t, first, 3])

    forward_line(0)
    own.wait()
    for i in range(5):
        loads[i].wait()
    weights_in = (w_query, w_key, w_value, w_gate)

    def project_line(t, second, which=(0, 1, 2, 3)):
        heads = [head_at(t, first, second) for first in range(4)]
        total = None
        pieces = []
        for h in heads:
            piece = gathered[h, t].astype(jnp.float32)
            if 1 in which:
                square = piece * piece
                total = square if total is None else total + square
            pieces.append((piece * attn_gain[pl.ds(h, 1), :]).astype(jnp.bfloat16))
        if 1 in which:
            if second == 0:
                squares[t] = total
            else:
                squares[t] += total
        gained = jnp.concatenate(pieces, axis=1)
        for i in which:
            weight = weights_in[i]
            deep = jnp.concatenate(
                [weight[pl.ds(pl.multiple_of(h * 128, 128), 128), :] for h in heads], axis=0
            )
            product = dot(gained, deep)
            if second == 0:
                acc[t, :, i * HERE : (i + 1) * HERE] = product
            else:
                acc[t, :, i * HERE : (i + 1) * HERE] += product

    project_line(0, 0)
    project_line(1, 0)
    for first in (3, 1, 2):
        forward_line(first)
    for t in range(2):
        project_line(t, 3)
        project_line(t, 1)
    for t in range(2):
        for first in range(4):
            arrived_in(part(block(t, first, 2), 0), second_in.at[t, first, 2])
            arrived_in(part(block(t, first, 2), 1), second_in.at[t, first, 3])
    for t in range(2):
        project_line(t, 2, (1, 2))

    def scale_of(t):
        mean_sq = jnp.sum(squares[t], axis=-1, keepdims=True) * (1.0 / WIDTH)
        return lax.rsqrt(mean_sq + epsilon)

    for t in range(2):
        scale = scale_of(t)
        keys[t] = jax.nn.silu(acc[t, :, HERE : 2 * HERE] * scale).astype(jnp.bfloat16)
        values[t] = jax.nn.silu(acc[t, :, 2 * HERE : 3 * HERE] * scale).astype(jnp.bfloat16)
        for h in range(2):
            states[t, h] = lax.dot_general(
                keys[t, :, h * DH : (h + 1) * DH],
                values[t, :, h * DH : (h + 1) * DH],
                (((0,), (0,)), ((), ())),
                preferred_element_type=jnp.float32,
            )
    pair_out[...] = states[1 - my_core].astype(jnp.bfloat16)
    pair = pltpu.make_async_remote_copy(
        src_ref=pair_out,
        dst_ref=pair_in,
        send_sem=state_out.at[0],
        recv_sem=state_in.at[0],
        device_id=(other_core, my_head),
        device_id_type=MESH,
    )
    pair.start()
    project_line(0, 2, (0, 3))
    project_line(1, 2, (0, 3))

    causal = lax.broadcasted_iota(jnp.int32, (BLOCK, BLOCK), 0) >= lax.broadcasted_iota(
        jnp.int32, (BLOCK, BLOCK), 1
    )

    def inner(t):
        queries = jax.nn.silu(acc[t, :, 0:HERE] * scale_of(t)).astype(jnp.bfloat16)
        gated[t] = queries
        for h in range(2):
            cols = slice(h * DH, (h + 1) * DH)
            scores = lax.dot_general(
                queries[:, cols],
                keys[t, :, cols],
                (((1,), (1,)), ((), ())),
                preferred_element_type=jnp.float32,
            )
            scores = jnp.where(causal, scores, 0.0).astype(jnp.bfloat16)
            mixed[t, :, cols] = dot(scores, values[t, :, cols])
        acc[t, :, 3 * HERE : 4 * HERE] = jax.nn.sigmoid(acc[t, :, 3 * HERE : 4 * HERE] * scale_of(t))

    pair.wait_recv()
    total_out[...] = (states[my_core] + pair_in[...].astype(jnp.float32)).astype(jnp.bfloat16)
    totals = [
        pltpu.make_async_remote_copy(
            src_ref=total_out,
            dst_ref=total_in.at[dz - 1],
            send_sem=state_out.at[dz],
            recv_sem=state_in.at[dz],
            device_id=(lax.rem(my_z + dz, 4) * 2 + my_core, my_head),
            device_id_type=MESH,
        )
        for dz in (1, 2, 3)
    ]
    for total in totals:
        total.start()
    inner(0)
    inner(1)
    base = jnp.zeros((2, DH, DH), jnp.float32)
    for dz in (1, 2, 3):
        totals[dz - 1].wait_recv()
        earlier_chip = jnp.where(my_z >= dz, 1.0, 0.0)
        base = base + earlier_chip * total_in[dz - 1].astype(jnp.float32)
    second_core = my_core.astype(jnp.float32)
    prefix_out[1] = (base + second_core * pair_in[...].astype(jnp.float32)).astype(jnp.bfloat16)
    prefix_out[0] = (base + (1.0 - second_core) * states[my_core]).astype(jnp.bfloat16)
    hand_over = pltpu.make_async_remote_copy(
        src_ref=prefix_out.at[0],
        dst_ref=prefix_in,
        send_sem=state_out.at[4],
        recv_sem=state_in.at[4],
        device_id=(other_core, my_head),
        device_id_type=MESH,
    )
    hand_over.start()
    for i in (6, 7):
        loads[i].wait()
    hand_over.wait_recv()

    for t in range(2):
        gate = acc[t, :, 3 * HERE : 4 * HERE]
        for h in range(2):
            cols = slice(h * DH, (h + 1) * DH)
            prefix = jnp.where(my_core == t, prefix_out[1, h], prefix_in[h])
            whole = mixed[t, :, cols] + dot(gated[t, :, cols], prefix)
            normed = rms_scale(whole, head_gain[h : h + 1, :])
            gated[t, :, cols] = (normed * gate[:, cols]).astype(jnp.bfloat16)
    for t in range(2):
        for j in range(4):
            cols = slice(j * 512, (j + 1) * 512)
            partial[t * BLOCK : (t + 1) * BLOCK, cols] = dot(gated[t], w_out[:, cols])

    def own_part(t, first, second, low, high):
        start = pl.multiple_of(head_at(t, first, second) * ROWS, ROWS)
        return partial[pl.ds(start, ROWS), t * WIDE + low : t * WIDE + high]

    for k in FAR_FIRST:
        for t in range(2):
            s1[t, k, 0] = own_part(t, k, 2, 0, PIECE).astype(jnp.bfloat16)
            push(s1.at[t, k, 0], r1.at[t, k, 0], t, 0, 1, sum_out.at[0], sum1_in.at[t, k, 0])
            s1[t, k, 1] = own_part(t, k, 2, PIECE, WIDE).astype(jnp.bfloat16)
            push(s1.at[t, k, 1], r1.at[t, k, 1], t, 0, 3, sum_out.at[0], sum1_in.at[t, k, 1])
    for k in FAR_FIRST:
        for t in range(2):
            arrived_in(r1.at[t, k, 0], sum1_in.at[t, k, 0])
            s2[t, k, 0, :, 0:PIECE] = (
                own_part(t, k, 1, 0, PIECE) + r1[t, k, 0].astype(jnp.float32)
            ).astype(jnp.bfloat16)
            s2[t, k, 0, :, PIECE:WIDE] = own_part(t, k, 1, PIECE, WIDE).astype(jnp.bfloat16)
            push(s2.at[t, k, 0], r2.at[t, k, 0], t, 0, 1, sum_out.at[1], sum2_in.at[t, k, 0])
            arrived_in(r1.at[t, k, 1], sum1_in.at[t, k, 1])
            s2[t, k, 1, :, 0:PIECE] = own_part(t, k, 3, 0, PIECE).astype(jnp.bfloat16)
            s2[t, k, 1, :, PIECE:WIDE] = (
                own_part(t, k, 3, PIECE, WIDE) + r1[t, k, 1].astype(jnp.float32)
            ).astype(jnp.bfloat16)
            push(s2.at[t, k, 1], r2.at[t, k, 1], t, 0, 3, sum_out.at[1], sum2_in.at[t, k, 1])
    for k in FAR_FIRST:
        for t in range(2):
            arrived_in(r2.at[t, k, 0], sum2_in.at[t, k, 0])
            arrived_in(r2.at[t, k, 1], sum2_in.at[t, k, 1])
            line_sum = (
                own_part(t, k, 0, 0, WIDE)
                + r2[t, k, 0].astype(jnp.float32)
                + r2[t, k, 1].astype(jnp.float32)
            )
            if k == 0:
                near_sum[t] = line_sum
            else:
                s3[t, k - 1] = line_sum.astype(jnp.bfloat16)
                push(s3.at[t, k - 1], r3.at[t, k - 1], t, k, 0, sum_out.at[2], sum3_in.at[t, k - 1])
    own_start = pl.multiple_of(lax.rem(my_head, 8) * ROWS, ROWS)
    for j in range(TILES):
        residual_ref[0, :, j * 128 : (j + 1) * 128] = gathered[
            j, my_head // 8, pl.ds(own_start, ROWS), :
        ].astype(jnp.float32)
    for t in range(2):
        total = near_sum[t]
        for k in range(3):
            arrived_in(r3.at[t, k], sum3_in.at[t, k])
            total = total + r3[t, k].astype(jnp.float32)
        residual_ref[0, :, t * WIDE : (t + 1) * WIDE] += total

    for i in (8, 9):
        loads[i].wait()
    moe_in = rms_scale(residual_ref[0], moe_gain[...]).astype(jnp.bfloat16)
    for j in range(0, TILES, 2):
        picked = dot(select[...], moe_in[:, j * 128 : (j + 2) * 128])
        for c in range(SLOTS):
            for half in range(2):
                spread[pl.ds(c * TILES + j + half, DEVS, CHUNK), :] = picked[
                    c * DEVS : (c + 1) * DEVS, half * 128 : (half + 1) * 128
                ]
    def away(n, sign):
        i = lax.rem(n, 4)
        o = lax.rem(n // 4, SEQ)
        dy = lax.rem(i + n // MEMBERS, 4)
        x = lax.rem(my_x + 4 + sign * i, 4)
        y = lax.rem(my_y + 4 + sign * dy, 4)
        return (lax.rem(my_seq + SEQ + sign * o, SEQ), y * 4 + x)

    part_lines = MEMBERS * CHUNK
    for g in range(GROUPS):
        members = pl.ds(g * MEMBERS, MEMBERS)
        outgoing[members] = (
            spread[g * part_lines : (g + 1) * part_lines, :]
            .astype(jnp.bfloat16)
            .reshape(MEMBERS, CHUNK, 128)
        )
        if g == 0:
            pltpu.make_async_copy(outgoing.at[0], arrived.at[0], in_sem.at[0]).start()

        def send(n, carry):
            pltpu.make_async_remote_copy(
                src_ref=outgoing.at[n],
                dst_ref=arrived.at[n],
                send_sem=out_sem,
                recv_sem=in_sem.at[g],
                device_id=away(n, 1),
                device_id_type=MESH,
            ).start()
            return carry

        lax.fori_loop(max(1, g * MEMBERS), (g + 1) * MEMBERS, send, 0)

    logits = dot(moe_in, w_router[...])
    scores = match_ref[...] * jax.nn.sigmoid(logits)
    weights = jnp.transpose(scores / jnp.sum(scores, axis=1, keepdims=True))
    high = weights.astype(jnp.bfloat16)
    low = (weights - high.astype(jnp.float32)).astype(jnp.bfloat16)
    near_high = dot(permute[...], high)
    near_low = dot(permute[...], low)

    for i in (10, 11, 12):
        loads[i].wait()
    part_rows = MEMBERS * SLOTS
    for g in range(GROUPS):
        members = pl.ds(g * MEMBERS, MEMBERS)
        arrived_in(arrived.at[members], in_sem.at[g])
        spread[0:part_lines, :] = arrived[members].astype(jnp.float32).reshape(part_lines, 128)
        for j in range(TILES):
            rows[:, j * 128 : (j + 1) * 128] = spread[pl.ds(j, part_rows, TILES), :].astype(
                jnp.bfloat16
            )
        inputs = rows[...]
        hidden = (jax.nn.silu(dot(inputs, gate_w[...])) * dot(inputs, up_w[...])).astype(
            jnp.bfloat16
        )
        for j in range(0, TILES, 2):
            produced = dot(hidden, down_w[:, j * 128 : (j + 2) * 128])
            for half in range(2):
                spread[pl.ds(j + half, part_rows, TILES), :] = produced[
                    :, half * 128 : (half + 1) * 128
                ]
        result[members] = (
            spread[0:part_lines, :].astype(jnp.bfloat16).reshape(MEMBERS, CHUNK, 128)
        )
        if g == 0:
            pltpu.make_async_copy(result.at[0], returned.at[0], back_in_sem.at[0]).start()

        def send_back(n, carry):
            pltpu.make_async_remote_copy(
                src_ref=result.at[n],
                dst_ref=returned.at[n],
                send_sem=back_out_sem,
                recv_sem=back_in_sem.at[g],
                device_id=away(n, -1),
                device_id_type=MESH,
            ).start()
            return carry

        lax.fori_loop(max(1, g * MEMBERS), (g + 1) * MEMBERS, send_back, 0)

    def over_rows(a, b):
        return lax.dot_general(
            a, b, (((0,), (0,)), ((), ())), preferred_element_type=jnp.float32
        )

    for g in range(GROUPS):
        members = pl.ds(g * MEMBERS, MEMBERS)
        arrived_in(returned.at[members], back_in_sem.at[g])
        spread[0:part_lines, :] = returned[members].astype(jnp.float32).reshape(part_lines, 128)
        for c in range(SLOTS):
            for j in range(TILES):
                rows[c * MEMBERS : (c + 1) * MEMBERS, j * 128 : (j + 1) * 128] = spread[
                    pl.ds(c * TILES + j, MEMBERS, CHUNK), :
                ].astype(jnp.bfloat16)
        here = slice(g * MEMBERS, (g + 1) * MEMBERS)
        slots = slot_ref[here, :]
        parts = [
            jnp.concatenate(
                [jnp.where(slots == float(c), near[here, :], 0.0) for c in range(SLOTS)], axis=0
            ).astype(jnp.bfloat16)
            for near in (near_high, near_low)
        ]
        added = over_rows(parts[0], rows[...]) + over_rows(parts[1], rows[...])
        if g == 0:
            moe_ref[0] = added
        else:
            moe_ref[0] += added

    sent = gathered.at[pl.ds(0, HEAD - 1)]
    pltpu.make_async_copy(sent, sent, gather_out).wait()
    pair.wait_send()
    for total in totals:
        total.wait_send()
    hand_over.wait_send()
    for i, ref in enumerate((s1, s2, s3)):
        pltpu.make_async_copy(ref, ref, sum_out.at[i]).wait()
    sent = outgoing.at[pl.ds(0, DEVS - 1)]
    pltpu.make_async_copy(sent, sent, out_sem).wait()
    sent = result.at[pl.ds(0, DEVS - 1)]
    pltpu.make_async_copy(sent, sent, back_out_sem).wait()


def local(
    tokens,
    attn_gain,
    w_query,
    w_key,
    w_value,
    w_gate,
    head_gain,
    w_out,
    moe_gain,
    w_router,
    expert_picks,
    exp_gate,
    exp_up,
    exp_down,
):
    args = (
        tokens,
        attn_gain.reshape(TILES, 128),
        w_query,
        w_key,
        w_value,
        w_gate,
        head_gain.reshape(2, DH),
        w_out,
        moe_gain.reshape(1, WIDTH),
        w_router,
        jnp.transpose(expert_picks, (0, 2, 1)),
        exp_gate[0],
        exp_up[0],
        exp_down[0],
    )

    def half(*shape):
        return pltpu.VMEM(shape, jnp.bfloat16)

    def full(*shape):
        return pltpu.VMEM(shape, jnp.float32)

    def sems(*shape):
        return pltpu.SemaphoreType.DMA(shape)

    residual, moe_out = pl.pallas_call(
        layer_kernel,
        out_shape=(jax.ShapeDtypeStruct((1, ROWS, WIDTH), jnp.float32),) * 2,
        in_specs=[pl.BlockSpec(memory_space=pl.ANY)] * len(args),
        out_specs=(pl.BlockSpec(memory_space=pltpu.VMEM),) * 2,
        scratch_shapes=[pltpu.VMEM(a.shape, a.dtype) for a in args[1:]]
        + [
            half(HEAD, 2, BLOCK, 128),
            full(2, BLOCK, 128),
            full(2, BLOCK, 4 * HERE),
            half(2, BLOCK, HERE),
            half(2, BLOCK, HERE),
            full(2, 2, DH, DH),
            half(2, DH, DH),
            half(2, DH, DH),
            half(2, DH, DH),
            half(3, 2, DH, DH),
            half(2, 2, DH, DH),
            half(2, DH, DH),
            full(2, BLOCK, HERE),
            half(2, BLOCK, HERE),
            full(2 * BLOCK, WIDTH),
            full(2, ROWS, WIDE),
            half(2, 4, 2, ROWS, PIECE),
            half(2, 4, 2, ROWS, PIECE),
            half(2, 4, 2, ROWS, WIDE),
            half(2, 4, 2, ROWS, WIDE),
            half(2, 3, ROWS, WIDE),
            half(2, 3, ROWS, WIDE),
            half(DEVS * SLOTS, ROWS),
            full(ROWS, DEVS),
            half(DEVS, DEVS),
            full(DEVS, ROWS),
            full(DEVS * CHUNK, 128),
            half(DEVS, CHUNK, 128),
            half(DEVS, CHUNK, 128),
            half(DEVS, CHUNK, 128),
            half(DEVS, CHUNK, 128),
            half(MEMBERS * SLOTS, WIDTH),
            sems(13),
            sems(),
            sems(),
            sems(2, 4),
            sems(2, 4, 4),
            sems(5),
            sems(5),
            sems(3),
            sems(2, 4, 2),
            sems(2, 4, 2),
            sems(2, 3),
            sems(),
            sems(GROUPS),
            sems(),
            sems(GROUPS),
        ],
        compiler_params=pltpu.CompilerParams(
            collective_id=1, has_side_effects=True, vmem_limit_bytes=56 * 1024 * 1024
        ),
        cost_estimate=pl.CostEstimate(
            flops=7 << 30, bytes_accessed=20 << 20, transcendentals=0
        ),
    )(*args)
    return residual + moe_out


def solution(mesh):
    placed = (
        P(None, "seq", "head"),
        P(),
        P(None, "head"),
        P(None, "head"),
        P(None, "head"),
        P(None, "head"),
        P("head"),
        P("head", None),
        P(),
        P(),
        P("seq", "head", None),
        P(("seq", "head"), None, None),
        P(("seq", "head"), None, None),
        P(("seq", "head"), None, None),
    )
    return jax.shard_map(
        local, mesh=mesh, in_specs=placed, out_specs=P("seq", "head", None), check_vma=False
    )
```

```python
import jax
import jax.numpy as jnp
from jax import lax
from jax.experimental import pallas as pl
from jax.experimental.pallas import tpu as pltpu
from jax.sharding import PartitionSpec as P

MESH = pl.DeviceIdType.MESH
SEQ = 8
HEAD = 16
DEVS = SEQ * HEAD
DH = 128
BLOCK = 256
ROWS = 32
TOP = 8
SLOTS = 3
WIDTH = 2048
HIDDEN = 768
TILES = WIDTH // 128
CHUNK = SLOTS * TILES
GROUPS = 4
MEMBERS = DEVS // GROUPS
HERE = 256
WIDE = WIDTH // 2
PIECE = WIDE // 2
FAR_FIRST = (2, 3, 1, 0)

epsilon = 1e-06


def rms_scale(values, gain_vec):
    mean_sq = jnp.mean(values * values, axis=-1, keepdims=True)
    return values * lax.rsqrt(mean_sq + epsilon) * gain_vec


def dot(a, b):
    return jnp.dot(a, b, preferred_element_type=jnp.float32)


def arrived_in(ref, sem):
    pltpu.make_async_copy(ref, ref, sem).wait()


def layer_kernel(
    tokens_hbm,
    attn_gain_hbm,
    query_hbm,
    key_hbm,
    value_hbm,
    gate_hbm,
    head_gain_hbm,
    out_hbm,
    moe_gain_hbm,
    router_hbm,
    picks_hbm,
    exp_gate_hbm,
    exp_up_hbm,
    exp_down_hbm,
    residual_ref,
    moe_ref,
    attn_gain,
    w_query,
    w_key,
    w_value,
    w_gate,
    head_gain,
    w_out,
    moe_gain,
    w_router,
    picks_ref,
    gate_w,
    up_w,
    down_w,
    gathered,
    squares,
    acc,
    keys,
    values,
    states,
    pair_out,
    pair_in,
    total_out,
    total_in,
    prefix_out,
    prefix_in,
    mixed,
    gated,
    partial,
    near_sum,
    s1,
    r1,
    s2,
    r2,
    s3,
    r3,
    select,
    match_ref,
    permute,
    slot_ref,
    spread,
    outgoing,
    arrived,
    result,
    returned,
    rows,
    load_sem,
    own_sem,
    gather_out,
    first_in,
    second_in,
    state_out,
    state_in,
    sum_out,
    sum1_in,
    sum2_in,
    sum3_in,
    out_sem,
    in_sem,
    back_out_sem,
    back_in_sem,
):
    my_seq = lax.axis_index("seq")
    my_head = lax.axis_index("head")
    me = my_seq * HEAD + my_head
    my_x = lax.rem(my_head, 4)
    my_y = my_head // 4
    my_z = my_seq // 2
    my_core = lax.rem(my_seq, 2)
    other_core = my_seq + 1 - 2 * my_core

    def head_at(t, first, second):
        dx, dy = (first, second) if t == 0 else (second, first)
        return lax.rem(my_y + dy, 4) * 4 + lax.rem(my_x + dx, 4)

    barrier = pltpu.get_barrier_semaphore()
    partners = [(my_seq, head_at(0, 1, 0)), (my_seq, head_at(0, 3, 0))]
    partners += [(my_seq, head_at(0, 0, 1)), (my_seq, head_at(0, 0, 3))]
    partners += [(my_seq, head_at(0, 2, 0)), (my_seq, head_at(0, 0, 2))]
    partners += [(other_core, my_head)]
    partners += [(lax.rem(my_z + dz, 4) * 2 + my_core, my_head) for dz in (1, 2, 3)]
    for partner in partners:
        pl.semaphore_signal(barrier, inc=1, device_id=partner, device_id_type=MESH)
    own = pltpu.make_async_copy(tokens_hbm, gathered.at[my_head], own_sem)
    own.start()
    loads = [
        pltpu.make_async_copy(hbm, vmem, load_sem.at[i])
        for i, (hbm, vmem) in enumerate(
            (
                (attn_gain_hbm, attn_gain),
                (query_hbm, w_query),
                (key_hbm, w_key),
                (value_hbm, w_value),
                (gate_hbm, w_gate),
                (picks_hbm, picks_ref),
                (head_gain_hbm, head_gain),
                (out_hbm, w_out),
                (moe_gain_hbm, moe_gain),
                (router_hbm, w_router),
                (exp_gate_hbm, gate_w),
                (exp_up_hbm, up_w),
                (exp_down_hbm, down_w),
            )
        )
    ]
    for load in loads:
        load.start()
    pl.semaphore_wait(barrier, len(partners))

    def push(source, target, t, first, second, send_sem, recv_sem):
        pltpu.make_async_remote_copy(
            src_ref=source,
            dst_ref=target,
            send_sem=send_sem,
            recv_sem=recv_sem,
            device_id=(my_seq, head_at(t, first, second)),
            device_id_type=MESH,
        ).start()

    def block(t, first, second):
        return gathered.at[head_at(t, first, second), t]

    def part(ref, i):
        return ref.at[pl.ds(i * BLOCK // 2, BLOCK // 2)]

    def pass_on(t, first, source):
        here = block(t, first, 0)
        push(source, here, t, 0, 1, gather_out, second_in.at[t, first, 0])
        push(source, here, t, 0, 3, gather_out, second_in.at[t, first, 1])

    for t in range(2):
        for step in (1, 3, 2):
            push(tokens_hbm.at[t], block(t, 0, 0), t, step, 0, gather_out, first_in.at[t, 4 - step])
    for t in range(2):
        pass_on(t, 0, tokens_hbm.at[t])

    loads[5].wait()
    line = lax.broadcasted_iota(jnp.int32, (DEVS, ROWS), 0)
    offset = line // MEMBERS
    step_x = lax.rem(line, 4)
    expert_x = lax.rem(my_x + step_x, 4)
    expert_y = lax.rem(my_y + step_x + offset, 4)
    expert_seq = lax.rem(my_seq + lax.rem(line // 4 + 2 * step_x, SEQ), SEQ)
    expert = expert_seq * HEAD + expert_y * 4 + expert_x
    picks = picks_ref[0]
    match_t = jnp.zeros((DEVS, ROWS), jnp.float32)
    near_t = jnp.zeros((DEVS, ROWS), jnp.float32)
    for k in range(TOP):
        match_t = match_t + jnp.where(picks[k : k + 1, :] == line, 1.0, 0.0)
        near_t = near_t + jnp.where(picks[k : k + 1, :] == expert, 1.0, 0.0)
    row_i = lax.broadcasted_iota(jnp.int32, (ROWS, ROWS), 0)
    col_i = lax.broadcasted_iota(jnp.int32, (ROWS, ROWS), 1)
    earlier_t = jnp.where(row_i < col_i, 1.0, 0.0).astype(jnp.bfloat16)
    before_t = dot(near_t.astype(jnp.bfloat16), earlier_t)
    match_ref[...] = jnp.transpose(match_t)
    slot_ref[...] = jnp.where(near_t > 0.0, before_t, float(SLOTS))
    all_lanes = lax.broadcasted_iota(jnp.int32, (DEVS, DEVS), 1)
    permute[...] = jnp.where(expert[:, 0:1] == all_lanes, 1.0, 0.0).astype(jnp.bfloat16)
    for g in range(GROUPS):
        here = slice(g * MEMBERS, (g + 1) * MEMBERS)
        for c in range(SLOTS):
            start = (g * SLOTS + c) * MEMBERS
            select[start : start + MEMBERS, :] = jnp.where(
                before_t[here, :] == float(c), near_t[here, :], 0.0
            ).astype(jnp.bfloat16)

    for first in (3, 1, 2):
        for t in range(2):
            arrived_in(block(t, first, 0), first_in.at[t, first])
            pass_on(t, first, block(t, first, 0))

    def forward_line(first):
        for t in range(2):
            lower = block(t, first, 3)
            arrived_in(lower, second_in.at[t, first, 0])
            push(part(lower, 0), part(lower, 0), t, 0, 1, gather_out, second_in.at[t, first, 2])
            upper = block(t, first, 1)
            arrived_in(upper, second_in.at[t, first, 1])
            push(part(upper, 1), part(upper, 1), t, 0, 3, gather_out, second_in.at[t, first, 3])

    forward_line(0)
    own.wait()
    for i in range(5):
        loads[i].wait()
    weights_in = (w_query, w_key, w_value, w_gate)

    def project_line(t, second, which=(0, 1, 2, 3)):
        heads = [head_at(t, first, second) for first in range(4)]
        total = None
        pieces = []
        for h in heads:
            piece = gathered[h, t].astype(jnp.float32)
            if 1 in which:
                square = piece * piece
                total = square if total is None else total + square
            pieces.append((piece * attn_gain[pl.ds(h, 1), :]).astype(jnp.bfloat16))
        if 1 in which:
            if second == 0:
                squares[t] = total
            else:
                squares[t] += total
        gained = jnp.concatenate(pieces, axis=1)
        for i in which:
            weight = weights_in[i]
            deep = jnp.concatenate(
                [weight[pl.ds(pl.multiple_of(h * 128, 128), 128), :] for h in heads], axis=0
            )
            product = dot(gained, deep)
            if second == 0:
                acc[t, :, i * HERE : (i + 1) * HERE] = product
            else:
                acc[t, :, i * HERE : (i + 1) * HERE] += product

    project_line(0, 0)
    project_line(1, 0)
    for first in (3, 1, 2):
        forward_line(first)
    for t in range(2):
        project_line(t, 3)
        project_line(t, 1)
    for t in range(2):
        for first in range(4):
            arrived_in(part(block(t, first, 2), 0), second_in.at[t, first, 2])
            arrived_in(part(block(t, first, 2), 1), second_in.at[t, first, 3])
    for t in range(2):
        project_line(t, 2, (1, 2))

    def scale_of(t):
        mean_sq = jnp.sum(squares[t], axis=-1, keepdims=True) * (1.0 / WIDTH)
        return lax.rsqrt(mean_sq + epsilon)

    for t in range(2):
        scale = scale_of(t)
        keys[t] = jax.nn.silu(acc[t, :, HERE : 2 * HERE] * scale).astype(jnp.bfloat16)
        values[t] = jax.nn.silu(acc[t, :, 2 * HERE : 3 * HERE] * scale).astype(jnp.bfloat16)
        for h in range(2):
            states[t, h] = lax.dot_general(
                keys[t, :, h * DH : (h + 1) * DH],
                values[t, :, h * DH : (h + 1) * DH],
                (((0,), (0,)), ((), ())),
                preferred_element_type=jnp.float32,
            )
    pair_out[...] = states[1 - my_core].astype(jnp.bfloat16)
    pair = pltpu.make_async_remote_copy(
        src_ref=pair_out,
        dst_ref=pair_in,
        send_sem=state_out.at[0],
        recv_sem=state_in.at[0],
        device_id=(other_core, my_head),
        device_id_type=MESH,
    )
    pair.start()

    causal = lax.broadcasted_iota(jnp.int32, (BLOCK, BLOCK), 0) >= lax.broadcasted_iota(
        jnp.int32, (BLOCK, BLOCK), 1
    )

    def inner(t):
        queries = jax.nn.silu(acc[t, :, 0:HERE] * scale_of(t)).astype(jnp.bfloat16)
        gated[t] = queries
        for h in range(2):
            cols = slice(h * DH, (h + 1) * DH)
            scores = lax.dot_general(
                queries[:, cols],
                keys[t, :, cols],
                (((1,), (1,)), ((), ())),
                preferred_element_type=jnp.float32,
            )
            scores = jnp.where(causal, scores, 0.0).astype(jnp.bfloat16)
            mixed[t, :, cols] = dot(scores, values[t, :, cols])
        acc[t, :, 3 * HERE : 4 * HERE] = jax.nn.sigmoid(acc[t, :, 3 * HERE : 4 * HERE] * scale_of(t))

    pair.wait_recv()
    total_out[...] = (states[my_core] + pair_in[...].astype(jnp.float32)).astype(jnp.bfloat16)
    totals = [
        pltpu.make_async_remote_copy(
            src_ref=total_out,
            dst_ref=total_in.at[dz - 1],
            send_sem=state_out.at[dz],
            recv_sem=state_in.at[dz],
            device_id=(lax.rem(my_z + dz, 4) * 2 + my_core, my_head),
            device_id_type=MESH,
        )
        for dz in (1, 2, 3)
    ]
    for total in totals:
        total.start()
    for t in range(2):
        project_line(t, 2, (0, 3))
        inner(t)
    base = jnp.zeros((2, DH, DH), jnp.float32)
    for dz in (1, 2, 3):
        totals[dz - 1].wait_recv()
        earlier_chip = jnp.where(my_z >= dz, 1.0, 0.0)
        base = base + earlier_chip * total_in[dz - 1].astype(jnp.float32)
    second_core = my_core.astype(jnp.float32)
    prefix_out[1] = (base + second_core * pair_in[...].astype(jnp.float32)).astype(jnp.bfloat16)
    prefix_out[0] = (base + (1.0 - second_core) * states[my_core]).astype(jnp.bfloat16)
    hand_over = pltpu.make_async_remote_copy(
        src_ref=prefix_out.at[0],
        dst_ref=prefix_in,
        send_sem=state_out.at[4],
        recv_sem=state_in.at[4],
        device_id=(other_core, my_head),
        device_id_type=MESH,
    )
    hand_over.start()
    for i in (6, 7):
        loads[i].wait()
    hand_over.wait_recv()

    for t in range(2):
        gate = acc[t, :, 3 * HERE : 4 * HERE]
        for h in range(2):
            cols = slice(h * DH, (h + 1) * DH)
            prefix = jnp.where(my_core == t, prefix_out[1, h], prefix_in[h])
            whole = mixed[t, :, cols] + dot(gated[t, :, cols], prefix)
            normed = rms_scale(whole, head_gain[h : h + 1, :])
            gated[t, :, cols] = (normed * gate[:, cols]).astype(jnp.bfloat16)
    for t in range(2):
        for j in range(4):
            cols = slice(j * 512, (j + 1) * 512)
            partial[t * BLOCK : (t + 1) * BLOCK, cols] = dot(gated[t], w_out[:, cols])

    def own_part(t, first, second, low, high):
        start = pl.multiple_of(head_at(t, first, second) * ROWS, ROWS)
        return partial[pl.ds(start, ROWS), t * WIDE + low : t * WIDE + high]

    for k in FAR_FIRST:
        for t in range(2):
            s1[t, k, 0] = own_part(t, k, 2, 0, PIECE).astype(jnp.bfloat16)
            push(s1.at[t, k, 0], r1.at[t, k, 0], t, 0, 1, sum_out.at[0], sum1_in.at[t, k, 0])
            s1[t, k, 1] = own_part(t, k, 2, PIECE, WIDE).astype(jnp.bfloat16)
            push(s1.at[t, k, 1], r1.at[t, k, 1], t, 0, 3, sum_out.at[0], sum1_in.at[t, k, 1])
    for k in FAR_FIRST:
        for t in range(2):
            arrived_in(r1.at[t, k, 0], sum1_in.at[t, k, 0])
            s2[t, k, 0, :, 0:PIECE] = (
                own_part(t, k, 1, 0, PIECE) + r1[t, k, 0].astype(jnp.float32)
            ).astype(jnp.bfloat16)
            s2[t, k, 0, :, PIECE:WIDE] = own_part(t, k, 1, PIECE, WIDE).astype(jnp.bfloat16)
            push(s2.at[t, k, 0], r2.at[t, k, 0], t, 0, 1, sum_out.at[1], sum2_in.at[t, k, 0])
            arrived_in(r1.at[t, k, 1], sum1_in.at[t, k, 1])
            s2[t, k, 1, :, 0:PIECE] = own_part(t, k, 3, 0, PIECE).astype(jnp.bfloat16)
            s2[t, k, 1, :, PIECE:WIDE] = (
                own_part(t, k, 3, PIECE, WIDE) + r1[t, k, 1].astype(jnp.float32)
            ).astype(jnp.bfloat16)
            push(s2.at[t, k, 1], r2.at[t, k, 1], t, 0, 3, sum_out.at[1], sum2_in.at[t, k, 1])
    for k in FAR_FIRST:
        for t in range(2):
            arrived_in(r2.at[t, k, 0], sum2_in.at[t, k, 0])
            arrived_in(r2.at[t, k, 1], sum2_in.at[t, k, 1])
            line_sum = (
                own_part(t, k, 0, 0, WIDE)
                + r2[t, k, 0].astype(jnp.float32)
                + r2[t, k, 1].astype(jnp.float32)
            )
            if k == 0:
                near_sum[t] = line_sum
            else:
                s3[t, k - 1] = line_sum.astype(jnp.bfloat16)
                push(s3.at[t, k - 1], r3.at[t, k - 1], t, k, 0, sum_out.at[2], sum3_in.at[t, k - 1])
    own_start = pl.multiple_of(lax.rem(my_head, 8) * ROWS, ROWS)
    for j in range(TILES):
        residual_ref[0, :, j * 128 : (j + 1) * 128] = gathered[
            j, my_head // 8, pl.ds(own_start, ROWS), :
        ].astype(jnp.float32)
    for t in range(2):
        total = near_sum[t]
        for k in range(3):
            arrived_in(r3.at[t, k], sum3_in.at[t, k])
            total = total + r3[t, k].astype(jnp.float32)
        residual_ref[0, :, t * WIDE : (t + 1) * WIDE] += total

    for i in (8, 9):
        loads[i].wait()
    moe_in = rms_scale(residual_ref[0], moe_gain[...]).astype(jnp.bfloat16)
    def away(n, sign):
        i = lax.rem(n, 4)
        o = lax.rem(n // 4 + 2 * i, SEQ)
        dy = lax.rem(i + n // MEMBERS, 4)
        x = lax.rem(my_x + 4 + sign * i, 4)
        y = lax.rem(my_y + 4 + sign * dy, 4)
        return (lax.rem(my_seq + SEQ + sign * o, SEQ), y * 4 + x)

    part_lines = MEMBERS * CHUNK
    for g in range(GROUPS):
        members = pl.ds(g * MEMBERS, MEMBERS)
        chosen = select[g * MEMBERS * SLOTS : (g + 1) * MEMBERS * SLOTS, :]
        for j in range(0, TILES, 2):
            picked = dot(chosen, moe_in[:, j * 128 : (j + 2) * 128])
            for c in range(SLOTS):
                for half in range(2):
                    spread[pl.ds(g * part_lines + c * TILES + j + half, MEMBERS, CHUNK), :] = picked[
                        c * MEMBERS : (c + 1) * MEMBERS, half * 128 : (half + 1) * 128
                    ]
        outgoing[members] = (
            spread[g * part_lines : (g + 1) * part_lines, :]
            .astype(jnp.bfloat16)
            .reshape(MEMBERS, CHUNK, 128)
        )
        if g == 0:
            pltpu.make_async_copy(outgoing.at[0], arrived.at[0], in_sem.at[0]).start()

        def send(n, carry):
            pltpu.make_async_remote_copy(
                src_ref=outgoing.at[n],
                dst_ref=arrived.at[n],
                send_sem=out_sem,
                recv_sem=in_sem.at[g],
                device_id=away(n, 1),
                device_id_type=MESH,
            ).start()
            return carry

        lax.fori_loop(max(1, g * MEMBERS), (g + 1) * MEMBERS, send, 0)

    logits = dot(moe_in, w_router[...])
    scores = match_ref[...] * jax.nn.sigmoid(logits)
    weights = jnp.transpose(scores / jnp.sum(scores, axis=1, keepdims=True))
    high = weights.astype(jnp.bfloat16)
    low = (weights - high.astype(jnp.float32)).astype(jnp.bfloat16)
    near_high = dot(permute[...], high)
    near_low = dot(permute[...], low)

    for i in (10, 11, 12):
        loads[i].wait()
    part_rows = MEMBERS * SLOTS
    for g in range(GROUPS):
        members = pl.ds(g * MEMBERS, MEMBERS)
        arrived_in(arrived.at[members], in_sem.at[g])
        spread[0:part_lines, :] = arrived[members].astype(jnp.float32).reshape(part_lines, 128)
        for j in range(TILES):
            rows[:, j * 128 : (j + 1) * 128] = spread[pl.ds(j, part_rows, TILES), :].astype(
                jnp.bfloat16
            )
        inputs = rows[...]
        hidden = (jax.nn.silu(dot(inputs, gate_w[...])) * dot(inputs, up_w[...])).astype(
            jnp.bfloat16
        )
        for j in range(0, TILES, 2):
            produced = dot(hidden, down_w[:, j * 128 : (j + 2) * 128])
            for half in range(2):
                spread[pl.ds(j + half, part_rows, TILES), :] = produced[
                    :, half * 128 : (half + 1) * 128
                ]
        result[members] = (
            spread[0:part_lines, :].astype(jnp.bfloat16).reshape(MEMBERS, CHUNK, 128)
        )
        if g == 0:
            pltpu.make_async_copy(result.at[0], returned.at[0], back_in_sem.at[0]).start()

        def send_back(m, carry):
            n = (2 * g + 1) * MEMBERS - 1 - m + (1 if g == 0 else 0)
            pltpu.make_async_remote_copy(
                src_ref=result.at[n],
                dst_ref=returned.at[n],
                send_sem=back_out_sem,
                recv_sem=back_in_sem.at[g],
                device_id=away(n, -1),
                device_id_type=MESH,
            ).start()
            return carry

        lax.fori_loop(max(1, g * MEMBERS), (g + 1) * MEMBERS, send_back, 0)

    def over_rows(a, b):
        return lax.dot_general(
            a, b, (((0,), (0,)), ((), ())), preferred_element_type=jnp.float32
        )

    for g in range(GROUPS):
        members = pl.ds(g * MEMBERS, MEMBERS)
        arrived_in(returned.at[members], back_in_sem.at[g])
        spread[0:part_lines, :] = returned[members].astype(jnp.float32).reshape(part_lines, 128)
        for c in range(SLOTS):
            for j in range(TILES):
                rows[c * MEMBERS : (c + 1) * MEMBERS, j * 128 : (j + 1) * 128] = spread[
                    pl.ds(c * TILES + j, MEMBERS, CHUNK), :
                ].astype(jnp.bfloat16)
        here = slice(g * MEMBERS, (g + 1) * MEMBERS)
        slots = slot_ref[here, :]
        parts = [
            jnp.concatenate(
                [jnp.where(slots == float(c), near[here, :], 0.0) for c in range(SLOTS)], axis=0
            ).astype(jnp.bfloat16)
            for near in (near_high, near_low)
        ]
        added = over_rows(parts[0], rows[...]) + over_rows(parts[1], rows[...])
        if g == 0:
            moe_ref[0] = added
        else:
            moe_ref[0] += added

    sent = gathered.at[pl.ds(0, HEAD - 1)]
    pltpu.make_async_copy(sent, sent, gather_out).wait()
    pair.wait_send()
    for total in totals:
        total.wait_send()
    hand_over.wait_send()
    for i, ref in enumerate((s1, s2, s3)):
        pltpu.make_async_copy(ref, ref, sum_out.at[i]).wait()
    sent = outgoing.at[pl.ds(0, DEVS - 1)]
    pltpu.make_async_copy(sent, sent, out_sem).wait()
    sent = result.at[pl.ds(0, DEVS - 1)]
    pltpu.make_async_copy(sent, sent, back_out_sem).wait()


def local(
    tokens,
    attn_gain,
    w_query,
    w_key,
    w_value,
    w_gate,
    head_gain,
    w_out,
    moe_gain,
    w_router,
    expert_picks,
    exp_gate,
    exp_up,
    exp_down,
):
    args = (
        tokens,
        attn_gain.reshape(TILES, 128),
        w_query,
        w_key,
        w_value,
        w_gate,
        head_gain.reshape(2, DH),
        w_out,
        moe_gain.reshape(1, WIDTH),
        w_router,
        jnp.transpose(expert_picks, (0, 2, 1)),
        exp_gate[0],
        exp_up[0],
        exp_down[0],
    )

    def half(*shape):
        return pltpu.VMEM(shape, jnp.bfloat16)

    def full(*shape):
        return pltpu.VMEM(shape, jnp.float32)

    def sems(*shape):
        return pltpu.SemaphoreType.DMA(shape)

    residual, moe_out = pl.pallas_call(
        layer_kernel,
        out_shape=(jax.ShapeDtypeStruct((1, ROWS, WIDTH), jnp.float32),) * 2,
        in_specs=[pl.BlockSpec(memory_space=pl.ANY)] * len(args),
        out_specs=(pl.BlockSpec(memory_space=pltpu.VMEM),) * 2,
        scratch_shapes=[pltpu.VMEM(a.shape, a.dtype) for a in args[1:]]
        + [
            half(HEAD, 2, BLOCK, 128),
            full(2, BLOCK, 128),
            full(2, BLOCK, 4 * HERE),
            half(2, BLOCK, HERE),
            half(2, BLOCK, HERE),
            full(2, 2, DH, DH),
            half(2, DH, DH),
            half(2, DH, DH),
            half(2, DH, DH),
            half(3, 2, DH, DH),
            half(2, 2, DH, DH),
            half(2, DH, DH),
            full(2, BLOCK, HERE),
            half(2, BLOCK, HERE),
            full(2 * BLOCK, WIDTH),
            full(2, ROWS, WIDE),
            half(2, 4, 2, ROWS, PIECE),
            half(2, 4, 2, ROWS, PIECE),
            half(2, 4, 2, ROWS, WIDE),
            half(2, 4, 2, ROWS, WIDE),
            half(2, 3, ROWS, WIDE),
            half(2, 3, ROWS, WIDE),
            half(DEVS * SLOTS, ROWS),
            full(ROWS, DEVS),
            half(DEVS, DEVS),
            full(DEVS, ROWS),
            full(DEVS * CHUNK, 128),
            half(DEVS, CHUNK, 128),
            half(DEVS, CHUNK, 128),
            half(DEVS, CHUNK, 128),
            half(DEVS, CHUNK, 128),
            half(MEMBERS * SLOTS, WIDTH),
            sems(13),
            sems(),
            sems(),
            sems(2, 4),
            sems(2, 4, 4),
            sems(5),
            sems(5),
            sems(3),
            sems(2, 4, 2),
            sems(2, 4, 2),
            sems(2, 3),
            sems(),
            sems(GROUPS),
            sems(),
            sems(GROUPS),
        ],
        compiler_params=pltpu.CompilerParams(
            collective_id=1, has_side_effects=True, vmem_limit_bytes=56 * 1024 * 1024
        ),
        cost_estimate=pl.CostEstimate(
            flops=7 << 30, bytes_accessed=20 << 20, transcendentals=0
        ),
    )(*args)
    return residual + moe_out


def solution(mesh):
    placed = (
        P(None, "seq", "head"),
        P(),
        P(None, "head"),
        P(None, "head"),
        P(None, "head"),
        P(None, "head"),
        P("head"),
        P("head", None),
        P(),
        P(),
        P("seq", "head", None),
        P(("seq", "head"), None, None),
        P(("seq", "head"), None, None),
        P(("seq", "head"), None, None),
    )
    return jax.shard_map(
        local, mesh=mesh, in_specs=placed, out_specs=P("seq", "head", None), check_vma=False
    )
```

```python
import jax
import jax.numpy as jnp
from jax import lax
from jax.experimental import pallas as pl
from jax.experimental.pallas import tpu as pltpu
from jax.sharding import PartitionSpec as P

MESH = pl.DeviceIdType.MESH
SEQ = 8
HEAD = 16
DEVS = SEQ * HEAD
DH = 128
BLOCK = 256
ROWS = 32
TOP = 8
SLOTS = 3
WIDTH = 2048
HIDDEN = 768
TILES = WIDTH // 128
CHUNK = SLOTS * TILES
GROUPS = 4
MEMBERS = DEVS // GROUPS
HERE = 256
WIDE = WIDTH // 2
PIECE = WIDE // 2
FAR_FIRST = (2, 3, 1, 0)

epsilon = 1e-06


def rms_scale(values, gain_vec):
    mean_sq = jnp.mean(values * values, axis=-1, keepdims=True)
    return values * lax.rsqrt(mean_sq + epsilon) * gain_vec


def dot(a, b):
    return jnp.dot(a, b, preferred_element_type=jnp.float32)


def arrived_in(ref, sem):
    pltpu.make_async_copy(ref, ref, sem).wait()


def layer_kernel(
    tokens_hbm,
    attn_gain_hbm,
    query_hbm,
    key_hbm,
    value_hbm,
    gate_hbm,
    head_gain_hbm,
    out_hbm,
    moe_gain_hbm,
    router_hbm,
    picks_hbm,
    exp_gate_hbm,
    exp_up_hbm,
    exp_down_hbm,
    moe_ref,
    attn_gain,
    w_query,
    w_key,
    w_value,
    w_gate,
    head_gain,
    w_out,
    moe_gain,
    w_router,
    picks_ref,
    gate_w,
    up_w,
    down_w,
    gathered,
    squares,
    acc,
    keys,
    values,
    states,
    pair_out,
    pair_in,
    total_out,
    total_in,
    prefix_out,
    prefix_in,
    mixed,
    gated,
    partial,
    near_sum,
    s1,
    r1,
    s2,
    r2,
    s3,
    r3,
    select,
    match_ref,
    permute,
    slot_ref,
    residual_ref,
    spread,
    outgoing,
    arrived,
    result,
    returned,
    rows,
    load_sem,
    own_sem,
    gather_out,
    first_in,
    second_in,
    state_out,
    state_in,
    sum_out,
    sum1_in,
    sum2_in,
    sum3_in,
    out_sem,
    in_sem,
    back_out_sem,
    back_in_sem,
):
    my_seq = lax.axis_index("seq")
    my_head = lax.axis_index("head")
    me = my_seq * HEAD + my_head
    my_x = lax.rem(my_head, 4)
    my_y = my_head // 4
    my_z = my_seq // 2
    my_core = lax.rem(my_seq, 2)
    other_core = my_seq + 1 - 2 * my_core

    def head_at(t, first, second):
        dx, dy = (first, second) if t == 0 else (second, first)
        return lax.rem(my_y + dy, 4) * 4 + lax.rem(my_x + dx, 4)

    barrier = pltpu.get_barrier_semaphore()
    partners = [(my_seq, head_at(0, 1, 0)), (my_seq, head_at(0, 3, 0))]
    partners += [(my_seq, head_at(0, 0, 1)), (my_seq, head_at(0, 0, 3))]
    partners += [(my_seq, head_at(0, 2, 0)), (my_seq, head_at(0, 0, 2))]
    partners += [(other_core, my_head)]
    partners += [(lax.rem(my_z + dz, 4) * 2 + my_core, my_head) for dz in (1, 2, 3)]
    for partner in partners:
        pl.semaphore_signal(barrier, inc=1, device_id=partner, device_id_type=MESH)
    own = pltpu.make_async_copy(tokens_hbm, gathered.at[my_head], own_sem)
    own.start()
    loads = [
        pltpu.make_async_copy(hbm, vmem, load_sem.at[i])
        for i, (hbm, vmem) in enumerate(
            (
                (attn_gain_hbm, attn_gain),
                (query_hbm, w_query),
                (key_hbm, w_key),
                (value_hbm, w_value),
                (gate_hbm, w_gate),
                (picks_hbm, picks_ref),
                (head_gain_hbm, head_gain),
                (out_hbm, w_out),
                (moe_gain_hbm, moe_gain),
                (router_hbm, w_router),
                (exp_gate_hbm, gate_w),
                (exp_up_hbm, up_w),
                (exp_down_hbm, down_w),
            )
        )
    ]
    for load in loads:
        load.start()
    pl.semaphore_wait(barrier, len(partners))

    def push(source, target, t, first, second, send_sem, recv_sem):
        pltpu.make_async_remote_copy(
            src_ref=source,
            dst_ref=target,
            send_sem=send_sem,
            recv_sem=recv_sem,
            device_id=(my_seq, head_at(t, first, second)),
            device_id_type=MESH,
        ).start()

    def block(t, first, second):
        return gathered.at[head_at(t, first, second), t]

    def part(ref, i):
        return ref.at[pl.ds(i * BLOCK // 2, BLOCK // 2)]

    def pass_on(t, first, source):
        here = block(t, first, 0)
        push(source, here, t, 0, 1, gather_out, second_in.at[t, first, 0])
        push(source, here, t, 0, 3, gather_out, second_in.at[t, first, 1])

    for t in range(2):
        for step in (1, 3, 2):
            push(tokens_hbm.at[t], block(t, 0, 0), t, step, 0, gather_out, first_in.at[t, 4 - step])
    for t in range(2):
        pass_on(t, 0, tokens_hbm.at[t])

    loads[5].wait()
    line = lax.broadcasted_iota(jnp.int32, (DEVS, ROWS), 0)
    offset = line // MEMBERS
    step_x = lax.rem(line, 4)
    expert_x = lax.rem(my_x + step_x, 4)
    expert_y = lax.rem(my_y + step_x + offset, 4)
    expert_seq = lax.rem(my_seq + lax.rem(line // 4 + 2 * step_x, SEQ), SEQ)
    expert = expert_seq * HEAD + expert_y * 4 + expert_x
    picks = picks_ref[0]
    match_t = jnp.zeros((DEVS, ROWS), jnp.float32)
    near_t = jnp.zeros((DEVS, ROWS), jnp.float32)
    for k in range(TOP):
        match_t = match_t + jnp.where(picks[k : k + 1, :] == line, 1.0, 0.0)
        near_t = near_t + jnp.where(picks[k : k + 1, :] == expert, 1.0, 0.0)
    row_i = lax.broadcasted_iota(jnp.int32, (ROWS, ROWS), 0)
    col_i = lax.broadcasted_iota(jnp.int32, (ROWS, ROWS), 1)
    earlier_t = jnp.where(row_i < col_i, 1.0, 0.0).astype(jnp.bfloat16)
    before_t = dot(near_t.astype(jnp.bfloat16), earlier_t)
    match_ref[...] = jnp.transpose(match_t)
    slot_ref[...] = jnp.where(near_t > 0.0, before_t, float(SLOTS))
    all_lanes = lax.broadcasted_iota(jnp.int32, (DEVS, DEVS), 1)
    permute[...] = jnp.where(expert[:, 0:1] == all_lanes, 1.0, 0.0).astype(jnp.bfloat16)
    for g in range(GROUPS):
        here = slice(g * MEMBERS, (g + 1) * MEMBERS)
        for c in range(SLOTS):
            start = (g * SLOTS + c) * MEMBERS
            select[start : start + MEMBERS, :] = jnp.where(
                before_t[here, :] == float(c), near_t[here, :], 0.0
            ).astype(jnp.bfloat16)

    for first in (3, 1, 2):
        for t in range(2):
            arrived_in(block(t, first, 0), first_in.at[t, first])
            pass_on(t, first, block(t, first, 0))

    def forward_line(first):
        for t in range(2):
            lower = block(t, first, 3)
            arrived_in(lower, second_in.at[t, first, 0])
            push(part(lower, 0), part(lower, 0), t, 0, 1, gather_out, second_in.at[t, first, 2])
            upper = block(t, first, 1)
            arrived_in(upper, second_in.at[t, first, 1])
            push(part(upper, 1), part(upper, 1), t, 0, 3, gather_out, second_in.at[t, first, 3])

    forward_line(0)
    own.wait()
    for i in range(5):
        loads[i].wait()
    weights_in = (w_query, w_key, w_value, w_gate)

    def project_line(t, second, which=(0, 1, 2, 3)):
        heads = [head_at(t, first, second) for first in range(4)]
        total = None
        pieces = []
        for h in heads:
            piece = gathered[h, t].astype(jnp.float32)
            if 1 in which:
                square = piece * piece
                total = square if total is None else total + square
            pieces.append((piece * attn_gain[pl.ds(h, 1), :]).astype(jnp.bfloat16))
        if 1 in which:
            if second == 0:
                squares[t] = total
            else:
                squares[t] += total
        gained = jnp.concatenate(pieces, axis=1)
        for i in which:
            weight = weights_in[i]
            deep = jnp.concatenate(
                [weight[pl.ds(pl.multiple_of(h * 128, 128), 128), :] for h in heads], axis=0
            )
            product = dot(gained, deep)
            if second == 0:
                acc[t, :, i * HERE : (i + 1) * HERE] = product
            else:
                acc[t, :, i * HERE : (i + 1) * HERE] += product

    project_line(0, 0)
    project_line(1, 0)
    for first in (3, 1, 2):
        forward_line(first)
    for t in range(2):
        project_line(t, 3)
        project_line(t, 1)
    for t in range(2):
        for first in range(4):
            arrived_in(part(block(t, first, 2), 0), second_in.at[t, first, 2])
            arrived_in(part(block(t, first, 2), 1), second_in.at[t, first, 3])
    for t in range(2):
        project_line(t, 2, (1, 2))

    def scale_of(t):
        mean_sq = jnp.sum(squares[t], axis=-1, keepdims=True) * (1.0 / WIDTH)
        return lax.rsqrt(mean_sq + epsilon)

    for t in range(2):
        scale = scale_of(t)
        keys[t] = jax.nn.silu(acc[t, :, HERE : 2 * HERE] * scale).astype(jnp.bfloat16)
        values[t] = jax.nn.silu(acc[t, :, 2 * HERE : 3 * HERE] * scale).astype(jnp.bfloat16)
        for h in range(2):
            states[t, h] = lax.dot_general(
                keys[t, :, h * DH : (h + 1) * DH],
                values[t, :, h * DH : (h + 1) * DH],
                (((0,), (0,)), ((), ())),
                preferred_element_type=jnp.float32,
            )
    pair_out[...] = states[1 - my_core].astype(jnp.bfloat16)
    pair = pltpu.make_async_remote_copy(
        src_ref=pair_out,
        dst_ref=pair_in,
        send_sem=state_out.at[0],
        recv_sem=state_in.at[0],
        device_id=(other_core, my_head),
        device_id_type=MESH,
    )
    pair.start()

    causal = lax.broadcasted_iota(jnp.int32, (BLOCK, BLOCK), 0) >= lax.broadcasted_iota(
        jnp.int32, (BLOCK, BLOCK), 1
    )

    def inner(t):
        queries = jax.nn.silu(acc[t, :, 0:HERE] * scale_of(t)).astype(jnp.bfloat16)
        gated[t] = queries
        for h in range(2):
            cols = slice(h * DH, (h + 1) * DH)
            scores = lax.dot_general(
                queries[:, cols],
                keys[t, :, cols],
                (((1,), (1,)), ((), ())),
                preferred_element_type=jnp.float32,
            )
            scores = jnp.where(causal, scores, 0.0).astype(jnp.bfloat16)
            mixed[t, :, cols] = dot(scores, values[t, :, cols])
        acc[t, :, 3 * HERE : 4 * HERE] = jax.nn.sigmoid(acc[t, :, 3 * HERE : 4 * HERE] * scale_of(t))

    pair.wait_recv()
    total_out[...] = (states[my_core] + pair_in[...].astype(jnp.float32)).astype(jnp.bfloat16)
    totals = [
        pltpu.make_async_remote_copy(
            src_ref=total_out,
            dst_ref=total_in.at[dz - 1],
            send_sem=state_out.at[dz],
            recv_sem=state_in.at[dz],
            device_id=(lax.rem(my_z + dz, 4) * 2 + my_core, my_head),
            device_id_type=MESH,
        )
        for dz in (1, 2, 3)
    ]
    for total in totals:
        total.start()
    for t in range(2):
        project_line(t, 2, (0, 3))
        inner(t)
    base = jnp.zeros((2, DH, DH), jnp.float32)
    for dz in (1, 2, 3):
        totals[dz - 1].wait_recv()
        earlier_chip = jnp.where(my_z >= dz, 1.0, 0.0)
        base = base + earlier_chip * total_in[dz - 1].astype(jnp.float32)
    second_core = my_core.astype(jnp.float32)
    prefix_out[1] = (base + second_core * pair_in[...].astype(jnp.float32)).astype(jnp.bfloat16)
    prefix_out[0] = (base + (1.0 - second_core) * states[my_core]).astype(jnp.bfloat16)
    hand_over = pltpu.make_async_remote_copy(
        src_ref=prefix_out.at[0],
        dst_ref=prefix_in,
        send_sem=state_out.at[4],
        recv_sem=state_in.at[4],
        device_id=(other_core, my_head),
        device_id_type=MESH,
    )
    hand_over.start()
    for i in (6, 7):
        loads[i].wait()
    hand_over.wait_recv()

    for t in range(2):
        gate = acc[t, :, 3 * HERE : 4 * HERE]
        for h in range(2):
            cols = slice(h * DH, (h + 1) * DH)
            prefix = jnp.where(my_core == t, prefix_out[1, h], prefix_in[h])
            whole = mixed[t, :, cols] + dot(gated[t, :, cols], prefix)
            normed = rms_scale(whole, head_gain[h : h + 1, :])
            gated[t, :, cols] = (normed * gate[:, cols]).astype(jnp.bfloat16)
    for t in range(2):
        for j in range(4):
            cols = slice(j * 512, (j + 1) * 512)
            partial[t * BLOCK : (t + 1) * BLOCK, cols] = dot(gated[t], w_out[:, cols])

    def own_part(t, first, second, low, high):
        start = pl.multiple_of(head_at(t, first, second) * ROWS, ROWS)
        return partial[pl.ds(start, ROWS), t * WIDE + low : t * WIDE + high]

    for k in FAR_FIRST:
        for t in range(2):
            s1[t, k, 0] = own_part(t, k, 2, 0, PIECE).astype(jnp.bfloat16)
            push(s1.at[t, k, 0], r1.at[t, k, 0], t, 0, 1, sum_out.at[0], sum1_in.at[t, k, 0])
            s1[t, k, 1] = own_part(t, k, 2, PIECE, WIDE).astype(jnp.bfloat16)
            push(s1.at[t, k, 1], r1.at[t, k, 1], t, 0, 3, sum_out.at[0], sum1_in.at[t, k, 1])
    for k in FAR_FIRST:
        for t in range(2):
            arrived_in(r1.at[t, k, 0], sum1_in.at[t, k, 0])
            s2[t, k, 0, :, 0:PIECE] = (
                own_part(t, k, 1, 0, PIECE) + r1[t, k, 0].astype(jnp.float32)
            ).astype(jnp.bfloat16)
            s2[t, k, 0, :, PIECE:WIDE] = own_part(t, k, 1, PIECE, WIDE).astype(jnp.bfloat16)
            push(s2.at[t, k, 0], r2.at[t, k, 0], t, 0, 1, sum_out.at[1], sum2_in.at[t, k, 0])
            arrived_in(r1.at[t, k, 1], sum1_in.at[t, k, 1])
            s2[t, k, 1, :, 0:PIECE] = own_part(t, k, 3, 0, PIECE).astype(jnp.bfloat16)
            s2[t, k, 1, :, PIECE:WIDE] = (
                own_part(t, k, 3, PIECE, WIDE) + r1[t, k, 1].astype(jnp.float32)
            ).astype(jnp.bfloat16)
            push(s2.at[t, k, 1], r2.at[t, k, 1], t, 0, 3, sum_out.at[1], sum2_in.at[t, k, 1])
    for k in FAR_FIRST:
        for t in range(2):
            arrived_in(r2.at[t, k, 0], sum2_in.at[t, k, 0])
            arrived_in(r2.at[t, k, 1], sum2_in.at[t, k, 1])
            line_sum = (
                own_part(t, k, 0, 0, WIDE)
                + r2[t, k, 0].astype(jnp.float32)
                + r2[t, k, 1].astype(jnp.float32)
            )
            if k == 0:
                near_sum[t] = line_sum
            else:
                s3[t, k - 1] = line_sum.astype(jnp.bfloat16)
                push(s3.at[t, k - 1], r3.at[t, k - 1], t, k, 0, sum_out.at[2], sum3_in.at[t, k - 1])
    own_start = pl.multiple_of(lax.rem(my_head, 8) * ROWS, ROWS)
    for j in range(TILES):
        residual_ref[0, :, j * 128 : (j + 1) * 128] = gathered[
            j, my_head // 8, pl.ds(own_start, ROWS), :
        ].astype(jnp.float32)
    for t in range(2):
        total = near_sum[t]
        for k in range(3):
            arrived_in(r3.at[t, k], sum3_in.at[t, k])
            total = total + r3[t, k].astype(jnp.float32)
        residual_ref[0, :, t * WIDE : (t + 1) * WIDE] += total

    for i in (8, 9):
        loads[i].wait()
    moe_in = rms_scale(residual_ref[0], moe_gain[...]).astype(jnp.bfloat16)
    def away(n, sign):
        i = lax.rem(n, 4)
        o = lax.rem(n // 4 + 2 * i, SEQ)
        dy = lax.rem(i + n // MEMBERS, 4)
        x = lax.rem(my_x + 4 + sign * i, 4)
        y = lax.rem(my_y + 4 + sign * dy, 4)
        return (lax.rem(my_seq + SEQ + sign * o, SEQ), y * 4 + x)

    part_lines = MEMBERS * CHUNK
    for g in range(GROUPS):
        members = pl.ds(g * MEMBERS, MEMBERS)
        chosen = select[g * MEMBERS * SLOTS : (g + 1) * MEMBERS * SLOTS, :]
        for j in range(0, TILES, 2):
            picked = dot(chosen, moe_in[:, j * 128 : (j + 2) * 128])
            for c in range(SLOTS):
                for half in range(2):
                    spread[pl.ds(g * part_lines + c * TILES + j + half, MEMBERS, CHUNK), :] = picked[
                        c * MEMBERS : (c + 1) * MEMBERS, half * 128 : (half + 1) * 128
                    ]
        outgoing[members] = (
            spread[g * part_lines : (g + 1) * part_lines, :]
            .astype(jnp.bfloat16)
            .reshape(MEMBERS, CHUNK, 128)
        )
        if g == 0:
            pltpu.make_async_copy(outgoing.at[0], arrived.at[0], in_sem.at[0]).start()

        def send(n, carry):
            pltpu.make_async_remote_copy(
                src_ref=outgoing.at[n],
                dst_ref=arrived.at[n],
                send_sem=out_sem,
                recv_sem=in_sem.at[g],
                device_id=away(n, 1),
                device_id_type=MESH,
            ).start()
            return carry

        lax.fori_loop(max(1, g * MEMBERS), (g + 1) * MEMBERS, send, 0)

    logits = dot(moe_in, w_router[...])
    scores = match_ref[...] * jax.nn.sigmoid(logits)
    weights = jnp.transpose(scores / jnp.sum(scores, axis=1, keepdims=True))
    high = weights.astype(jnp.bfloat16)
    low = (weights - high.astype(jnp.float32)).astype(jnp.bfloat16)
    near_high = dot(permute[...], high)
    near_low = dot(permute[...], low)

    for i in (10, 11, 12):
        loads[i].wait()
    part_rows = MEMBERS * SLOTS
    for g in range(GROUPS):
        members = pl.ds(g * MEMBERS, MEMBERS)
        arrived_in(arrived.at[members], in_sem.at[g])
        spread[0:part_lines, :] = arrived[members].astype(jnp.float32).reshape(part_lines, 128)
        for j in range(TILES):
            rows[:, j * 128 : (j + 1) * 128] = spread[pl.ds(j, part_rows, TILES), :].astype(
                jnp.bfloat16
            )
        inputs = rows[...]
        hidden = (jax.nn.silu(dot(inputs, gate_w[...])) * dot(inputs, up_w[...])).astype(
            jnp.bfloat16
        )
        for j in range(0, TILES, 2):
            produced = dot(hidden, down_w[:, j * 128 : (j + 2) * 128])
            for half in range(2):
                spread[pl.ds(j + half, part_rows, TILES), :] = produced[
                    :, half * 128 : (half + 1) * 128
                ]
        result[members] = (
            spread[0:part_lines, :].astype(jnp.bfloat16).reshape(MEMBERS, CHUNK, 128)
        )
        if g == 0:
            pltpu.make_async_copy(result.at[0], returned.at[0], back_in_sem.at[0]).start()

        def send_back(m, carry):
            n = (2 * g + 1) * MEMBERS - 1 - m + (1 if g == 0 else 0)
            pltpu.make_async_remote_copy(
                src_ref=result.at[n],
                dst_ref=returned.at[n],
                send_sem=back_out_sem,
                recv_sem=back_in_sem.at[g],
                device_id=away(n, -1),
                device_id_type=MESH,
            ).start()
            return carry

        lax.fori_loop(max(1, g * MEMBERS), (g + 1) * MEMBERS, send_back, 0)

    def over_rows(a, b):
        return lax.dot_general(
            a, b, (((0,), (0,)), ((), ())), preferred_element_type=jnp.float32
        )

    for g in range(GROUPS):
        members = pl.ds(g * MEMBERS, MEMBERS)
        arrived_in(returned.at[members], back_in_sem.at[g])
        spread[0:part_lines, :] = returned[members].astype(jnp.float32).reshape(part_lines, 128)
        for c in range(SLOTS):
            for j in range(TILES):
                rows[c * MEMBERS : (c + 1) * MEMBERS, j * 128 : (j + 1) * 128] = spread[
                    pl.ds(c * TILES + j, MEMBERS, CHUNK), :
                ].astype(jnp.bfloat16)
        here = slice(g * MEMBERS, (g + 1) * MEMBERS)
        slots = slot_ref[here, :]
        parts = [
            jnp.concatenate(
                [jnp.where(slots == float(c), near[here, :], 0.0) for c in range(SLOTS)], axis=0
            ).astype(jnp.bfloat16)
            for near in (near_high, near_low)
        ]
        added = over_rows(parts[0], rows[...]) + over_rows(parts[1], rows[...])
        if g == 0:
            moe_ref[0] = residual_ref[0] + added
        else:
            moe_ref[0] += added

    sent = gathered.at[pl.ds(0, HEAD - 1)]
    pltpu.make_async_copy(sent, sent, gather_out).wait()
    pair.wait_send()
    for total in totals:
        total.wait_send()
    hand_over.wait_send()
    for i, ref in enumerate((s1, s2, s3)):
        pltpu.make_async_copy(ref, ref, sum_out.at[i]).wait()
    sent = outgoing.at[pl.ds(0, DEVS - 1)]
    pltpu.make_async_copy(sent, sent, out_sem).wait()
    sent = result.at[pl.ds(0, DEVS - 1)]
    pltpu.make_async_copy(sent, sent, back_out_sem).wait()


def local(
    tokens,
    attn_gain,
    w_query,
    w_key,
    w_value,
    w_gate,
    head_gain,
    w_out,
    moe_gain,
    w_router,
    expert_picks,
    exp_gate,
    exp_up,
    exp_down,
):
    args = (
        tokens,
        attn_gain.reshape(TILES, 128),
        w_query,
        w_key,
        w_value,
        w_gate,
        head_gain.reshape(2, DH),
        w_out,
        moe_gain.reshape(1, WIDTH),
        w_router,
        jnp.transpose(expert_picks, (0, 2, 1)),
        exp_gate[0],
        exp_up[0],
        exp_down[0],
    )

    def half(*shape):
        return pltpu.VMEM(shape, jnp.bfloat16)

    def full(*shape):
        return pltpu.VMEM(shape, jnp.float32)

    def sems(*shape):
        return pltpu.SemaphoreType.DMA(shape)

    (out,) = pl.pallas_call(
        layer_kernel,
        out_shape=(jax.ShapeDtypeStruct((1, ROWS, WIDTH), jnp.float32),),
        in_specs=[pl.BlockSpec(memory_space=pl.ANY)] * len(args),
        out_specs=(pl.BlockSpec(memory_space=pltpu.VMEM),),
        scratch_shapes=[pltpu.VMEM(a.shape, a.dtype) for a in args[1:]]
        + [
            half(HEAD, 2, BLOCK, 128),
            full(2, BLOCK, 128),
            full(2, BLOCK, 4 * HERE),
            half(2, BLOCK, HERE),
            half(2, BLOCK, HERE),
            full(2, 2, DH, DH),
            half(2, DH, DH),
            half(2, DH, DH),
            half(2, DH, DH),
            half(3, 2, DH, DH),
            half(2, 2, DH, DH),
            half(2, DH, DH),
            full(2, BLOCK, HERE),
            half(2, BLOCK, HERE),
            full(2 * BLOCK, WIDTH),
            full(2, ROWS, WIDE),
            half(2, 4, 2, ROWS, PIECE),
            half(2, 4, 2, ROWS, PIECE),
            half(2, 4, 2, ROWS, WIDE),
            half(2, 4, 2, ROWS, WIDE),
            half(2, 3, ROWS, WIDE),
            half(2, 3, ROWS, WIDE),
            half(DEVS * SLOTS, ROWS),
            full(ROWS, DEVS),
            half(DEVS, DEVS),
            full(DEVS, ROWS),
            full(1, ROWS, WIDTH),
            full(DEVS * CHUNK, 128),
            half(DEVS, CHUNK, 128),
            half(DEVS, CHUNK, 128),
            half(DEVS, CHUNK, 128),
            half(DEVS, CHUNK, 128),
            half(MEMBERS * SLOTS, WIDTH),
            sems(13),
            sems(),
            sems(),
            sems(2, 4),
            sems(2, 4, 4),
            sems(5),
            sems(5),
            sems(3),
            sems(2, 4, 2),
            sems(2, 4, 2),
            sems(2, 3),
            sems(),
            sems(GROUPS),
            sems(),
            sems(GROUPS),
        ],
        compiler_params=pltpu.CompilerParams(
            collective_id=1, has_side_effects=True, vmem_limit_bytes=56 * 1024 * 1024
        ),
        cost_estimate=pl.CostEstimate(
            flops=7 << 30, bytes_accessed=20 << 20, transcendentals=0
        ),
    )(*args)
    return out


def solution(mesh):
    placed = (
        P(None, "seq", "head"),
        P(),
        P(None, "head"),
        P(None, "head"),
        P(None, "head"),
        P(None, "head"),
        P("head"),
        P("head", None),
        P(),
        P(),
        P("seq", "head", None),
        P(("seq", "head"), None, None),
        P(("seq", "head"), None, None),
        P(("seq", "head"), None, None),
    )
    return jax.shard_map(
        local, mesh=mesh, in_specs=placed, out_specs=P("seq", "head", None), check_vma=False
    )
```
